32 devices in a mesh: groups: 2 (over y), dom: 4 (over z), rep: 4 (over x, core).
Axes of the slice: x: 2, y: 2, z: 4, core: 2. Of those that a mesh axis runs over, the one named last changes fastest.
Arguments:
- plan: int32 [4], P('dom'), may hold values from 0 to 3, as said below
- edge_lhs: int32 [8, 4096], P(('groups', 'dom'), 'rep'), parts along dimension 0, may hold values from 0 to 511
- edge_rhs: int32 [8, 4096], P(('groups', 'dom'), 'rep'), parts along dimension 0, may hold values from 0 to 255
- edge_rel: int32 [8, 4096], P(('groups', 'dom'), 'rep'), parts along dimension 0, may hold values from 0 to 511
- edge_count: int32 [32], P(('groups', 'dom', 'rep')), parts along dimension 0, may hold values from 1 to 1024, 8192 in all
- negatives: int32 [8, 8, 1000], P(('groups', 'dom'), 'rep'), parts along dimension 0, may hold values from 0 to 255
- emb: float32 [2048, 400], P(('groups', 'dom')), parts along dimension 0, may hold values from -2.4 to 2.4
- acc: float32 [2048], P(('groups', 'dom')), parts along dimension 0, may hold values from 0.2 to 2
- hot_emb: float32 [512, 400], P('groups'), parts along dimension 0, may hold values from -2.4 to 2.4
- hot_acc: float32 [512], P('groups'), parts along dimension 0, may hold values from 4 to 40
- relations: float32 [1024, 400], P('groups'), parts along dimension 0, may hold values from -4.2 to 4.2
Outputs:
- new_emb: float32 [2048, 400], P(('groups', 'dom')), parts along dimension 0
- new_acc: float32 [2048], P(('groups', 'dom')), parts along dimension 0
- new_hot: float32 [512, 400], P('groups'), parts along dimension 0
- new_hot_acc: float32 [512], P('groups'), parts along dimension 0
The draws below stay inside these ranges and needn't reach their ends.
There are 2 independent parts, one for each index of `groups`. The reference program is written for one: setup_inputs(seed, part) draws one part's arguments, and reference() takes and returns one part's arrays. A program takes and returns all parts, laid end to end along the dimension named above; an argument that names none is the same for every part. Nothing has to cross between parts.
Inputs may be any that keep to these rules, and one draw needn't show every extreme that they name: Worker w trains its own partition against partition plan[w] = (w + s) mod 4, for one s of 1 to 3 common to all workers and all groups. `edge_lhs`: values below 256 name rows of the worker's own partition, the others hot entity value - 256. `edge_count`: the live slots of a list come first. `negatives`: rows of the planned partition, repeats allowed.
All inputs are finite; a program needn't handle non-finite values. No bound on the sum of `edge_count` on one device may be relied on, other than what follows from the above.
Results may differ from the reference program's by a relative error of at most 0.004.
Values may be sent and summed in bfloat16 or wider, within the bound.
No kernel may reach another device: no remote copies, remote signals or barrier semaphores. Data moves between devices by JAX's collectives and lax.ppermute only.
A program may use at most 64 MiB of HBM per device.

```python
import math
import jax
import jax.numpy as jnp
import numpy as np
from jax import lax

D = 400
PR = 256
HOT = 256
REL = 512
NEGS = 1000
CH = 512
SPANS = 2
EDGES_DEV = 1024
PARTITIONS = 4
REPS = 4
SLOTS = 16
ENT = 1024


def draw_plan(key, part):
    key = jax.random.fold_in(key, 11)
    pieces = jax.random.randint(key, (16,), 0, 1048576, dtype=jnp.int32)
    offset = 1 + jnp.sum(pieces % (PARTITIONS - 1)) % (PARTITIONS - 1)
    return ((jnp.arange(PARTITIONS, dtype=jnp.int32) + offset) % PARTITIONS).astype(jnp.int32)


def set_ends(values, key, least, high):
    shape = values.shape
    spot = [jax.random.randint(jax.random.fold_in(key, axis), (), 0, shape[axis]) for axis in range(len(shape))]
    values = values.at[tuple(spot)].set(least)
    longest = shape.index(max(shape))
    spot[longest] = (spot[longest] + 1) % shape[longest]
    return values.at[tuple(spot)].set(high)


def block_scale(own_key, shape, shards, least, largest):
    def one(dim, shards_of):
        steps = jax.random.uniform(jax.random.fold_in(jax.random.fold_in(own_key, 6), dim), (shards_of,), jnp.float32, least / len(shards), largest / len(shards))
        return jnp.repeat(jnp.exp(steps), shape[dim] // shards_of).reshape((-1,) + (1,) * (len(shape) - dim - 1))

    level = one(*shards[0])
    for cut in shards[1:]:
        level = level * one(*cut)
    return level


def split_up(count, total, reach, skew):
    loads = [(1 << 20) // math.isqrt(grade ** skew) + 1 for grade in range(2, count + 1)]
    surplus, given = total - reach - (count - 1), [1] * (count - 1)
    while surplus > 0:
        movable = [i for i in range(count - 1) if given[i] < reach]
        mass, left = sum([loads[i] for i in movable]), surplus
        for i in movable:
            more = min(reach - given[i], max(1, left * loads[i] // mass), surplus)
            given[i] = given[i] + more
            surplus = surplus - more
    return np.array([reach] + given)


def ragged_sizes(rng, count, total, limit, lean):
    if count == 2:
        one = jax.random.randint(rng, (), max(1, total - limit), min(limit, total - 1) + 1)
        return jnp.stack([one, total - one])
    tallies = jnp.asarray(split_up(count, total, limit, lean), jnp.int32)
    couples = (count - 1) // 2
    donor, sink = tallies[1:1 + 2 * couples:2], tallies[2:2 + 2 * couples:2]
    room = jnp.minimum(donor - 1, limit - sink)
    moved = jax.random.randint(jax.random.fold_in(rng, 1), (couples,), 0, 1 << 20) % (room + 1)
    tallies = tallies.at[1:1 + 2 * couples:2].set(donor - moved).at[2:2 + 2 * couples:2].set(sink + moved)
    return tallies[jax.random.permutation(jax.random.fold_in(rng, 2), count)]


def gaussian(stream_key, extent, deviation, reach, cuts=(), kind=jnp.bfloat16):
    entries = jax.random.normal(stream_key, extent, jnp.float32) * deviation
    if len(cuts) > 0:
        entries = block_scale(stream_key, extent, cuts, -0.22, 0.18) * entries
    return jnp.clip(entries, min=-reach, max=reach).astype(kind)


def setup_inputs(seed: int = 0, part: int = 0) -> dict:
    splits = jax.random.split(jax.random.key(seed), 12)
    part_keys = jax.random.split(jax.random.fold_in(splits[11], part), 12)
    plan = draw_plan(jax.random.fold_in(splits[11], 71), part)
    edge_lhs = set_ends(jax.random.randint(part_keys[1], (PARTITIONS, REPS * EDGES_DEV), 0, PR + HOT), jax.random.fold_in(part_keys[1], 1), 0, (PR + HOT) - 1).astype(jnp.int32)
    edge_rhs = set_ends(jax.random.randint(part_keys[2], (PARTITIONS, REPS * EDGES_DEV), 0, PR), jax.random.fold_in(part_keys[2], 1), 0, PR - 1).astype(jnp.int32)
    edge_rel = set_ends(jax.random.randint(part_keys[3], (PARTITIONS, REPS * EDGES_DEV), 0, REL), jax.random.fold_in(part_keys[3], 1), 0, REL - 1).astype(jnp.int32)
    edge_count = ragged_sizes(part_keys[4], SLOTS, SLOTS * EDGES_DEV // 2, EDGES_DEV, 2).astype(jnp.int32)
    negatives = set_ends(jax.random.randint(part_keys[5], (PARTITIONS, REPS * SPANS, NEGS), 0, PR), jax.random.fold_in(part_keys[5], 1), 0, PR - 1).astype(jnp.int32)
    emb = gaussian(part_keys[6], (ENT, D), 0.4, 2.4, ((0, 4),), jnp.float32)
    acc = jnp.clip(jnp.exp(math.log(2.0) - 2.3025851 * jax.random.uniform(part_keys[7], (ENT,), jnp.float32) ** block_scale(part_keys[7], (ENT,), ((0, 4),), -0.2, 0.2)), 0.2, 2.0)
    hot_emb = gaussian(part_keys[8], (HOT, D), 0.4, 2.4, (), jnp.float32)
    hot_acc = jnp.clip(jnp.exp(jax.random.uniform(part_keys[9], (HOT,), jnp.float32, math.log(4.0), math.log(40.0))), 4.0, 40.0)
    relations = gaussian(part_keys[10], (REL, D), 0.7, 4.2, (), jnp.float32)
    return {"plan": plan, "edge_lhs": edge_lhs, "edge_rhs": edge_rhs, "edge_rel": edge_rel, "edge_count": edge_count, "negatives": negatives, "emb": emb, "acc": acc, "hot_emb": hot_emb, "hot_acc": hot_acc, "relations": relations}


LEARN_RATE = 0.5

def span_terms(left_bf, rel_rows, right_bf, negative_bf, mask):
    half = left_bf.shape[1] // 2
    left = left_bf.astype(jnp.float32)
    left_re, left_im = (left[:, :half], left[:, half:])
    rel_re, rel_im = (rel_rows[:, :half], rel_rows[:, half:])
    query = jnp.concatenate([left_re * rel_re - left_im * rel_im, left_re * rel_im + left_im * rel_re], 1).astype(jnp.bfloat16)
    query = lax.optimization_barrier(query)
    query_f = query.astype(jnp.float32)
    right_f = right_bf.astype(jnp.float32)
    positive = lax.optimization_barrier(jnp.sum(query_f * right_f, axis=1))
    scores = lax.dot_general(query, negative_bf, (((1,), (1,)), ((), ())), preferred_element_type=jnp.float32)
    grad_pos = -jax.nn.sigmoid(-positive) * mask
    grad_neg = (jax.nn.sigmoid(scores) * (mask / negative_bf.shape[0])[:, None]).astype(jnp.bfloat16)
    grad_query = grad_pos[:, None] * right_f + jnp.dot(grad_neg, negative_bf, preferred_element_type=jnp.float32)
    grad_right = grad_pos[:, None] * query_f
    grad_negative = lax.dot_general(grad_neg, query, (((0,), (0,)), ((), ())), preferred_element_type=jnp.float32)
    grad_re, grad_im = (grad_query[:, :half], grad_query[:, half:])
    grad_left = jnp.concatenate([grad_re * rel_re + grad_im * rel_im, grad_im * rel_re - grad_re * rel_im], 1)
    return (grad_left, grad_right, grad_negative)

def adagrad_rows(weights, accum, grad):
    accum_new = accum + lax.optimization_barrier(jnp.mean(grad * grad, axis=1))
    return (weights - LEARN_RATE * grad / jnp.sqrt(accum_new)[:, None], accum_new)

def reference(plan, edge_lhs, edge_rhs, edge_rel, edge_count, negatives, emb, acc, hot_emb, hot_acc, relations):
    total_rows = PR * PARTITIONS
    table = jnp.concatenate([emb, hot_emb], 0).astype(jnp.bfloat16)
    span_total = PARTITIONS * REPS * SPANS
    left_ids = edge_lhs.reshape(span_total, CH)
    right_ids = edge_rhs.reshape(span_total, CH)
    rel_ids = edge_rel.reshape(span_total, CH)
    negative_ids = negatives.reshape(span_total, NEGS)
    span_ids = jnp.arange(span_total, dtype=jnp.int32)
    workers = span_ids // (REPS * SPANS)
    lists = span_ids // SPANS
    within = span_ids % SPANS

    def step(grad, inputs):
        left_id, right_id, rel_id, negative_id, worker, list_id, block = inputs
        far_base = plan[worker] * PR
        left_rows = jnp.where(left_id < PR, worker * PR + left_id, total_rows + left_id - PR).astype(jnp.int32)
        right_rows = (far_base + right_id).astype(jnp.int32)
        negative_rows = (far_base + negative_id).astype(jnp.int32)
        positions = block * CH + jnp.arange(CH, dtype=jnp.int32)
        mask = (positions < edge_count[list_id]).astype(jnp.float32)
        grad_left, grad_right, grad_negative = span_terms(table[left_rows], relations[rel_id], table[right_rows], table[negative_rows], mask)
        grad = grad.at[left_rows].add(grad_left)
        grad = grad.at[right_rows].add(grad_right)
        grad = grad.at[negative_rows].add(grad_negative)
        return (grad, None)
    start = jnp.zeros((total_rows + HOT, D), jnp.float32)
    grad = lax.scan(step, start, (left_ids, right_ids, rel_ids, negative_ids, workers, lists, within))[0]
    new_emb, new_acc = adagrad_rows(emb, acc, grad[:total_rows])
    new_hot, new_hot_acc = adagrad_rows(hot_emb, hot_acc, grad[total_rows:])
    return (new_emb, new_acc, new_hot, new_hot_acc)
```

```python
import functools

import jax
import jax.numpy as jnp
from jax import lax
from jax.experimental import pallas as pl
from jax.experimental.pallas import tpu as pltpu
from jax.sharding import PartitionSpec as P

LEARN_RATE = 0.5
BF = jnp.bfloat16
F32 = jnp.float32
LHS, RHS, REL, NEG, LIVE = 0, 1, 2, 3, 5
VMEM_LIMIT = 48 * 1024 * 1024


def call(kernel, out_shape, scratch=(), smem=(), n_in=0, flops=0, nbytes=0, **kw):
    specs = [
        pl.BlockSpec(memory_space=pltpu.SMEM if i in smem else pltpu.VMEM) for i in range(n_in)
    ]
    return pl.pallas_call(
        kernel,
        out_shape=out_shape,
        in_specs=specs,
        scratch_shapes=list(scratch),
        compiler_params=pltpu.CompilerParams(vmem_limit_bytes=VMEM_LIMIT),
        cost_estimate=pl.CostEstimate(flops=flops, bytes_accessed=nbytes, transcendentals=0),
        **kw,
    )


def split(x):
    high = x.astype(BF)
    return high, (x - high.astype(F32)).astype(BF)


def dot_nt(a, b):
    return lax.dot_general(a, b, (((1,), (1,)), ((), ())), preferred_element_type=F32)


def dot_nn(a, b):
    return jnp.dot(a, b, preferred_element_type=F32)


def one_hot(ids, count):
    rows = lax.broadcasted_iota(jnp.int32, (count, ids.shape[1]), 0)
    return jnp.where(rows == ids, 1.0, 0.0).astype(BF)


def pack_kernel(count, emb, lhs, rhs, rel, neg, emb_bf, ids):
    emb_bf[...] = emb[...].astype(BF)
    width = ids.shape[1]
    ids[...] = jnp.full(ids.shape, -1, jnp.int32)
    ids[LHS : LHS + 1, :] = lhs[...]
    ids[RHS : RHS + 1, :] = rhs[...]
    ids[REL : REL + 1, :] = rel[...]
    ids[NEG : NEG + 2, 0 : neg.shape[2]] = neg[0]
    ids[LIVE : LIVE + 1, :] = jnp.full((1, width), count[0], jnp.int32)


def query_kernel(mine, other, emb, hot, rel, ids, query, rel_cols, counts, table, rel_parts):
    first = lax.axis_index("rep") // 2 == 0
    ids[0] = jnp.where(first, mine[...], other[...])
    ids[1] = jnp.where(first, other[...], mine[...])
    rows = emb.shape[1]
    n_rel = rel.shape[1]
    table[:, :rows] = emb[...].astype(BF)
    table[:, rows:] = hot[...].astype(BF)
    high, low = split(rel[...])
    rel_parts[:, :n_rel] = high
    rel_parts[:, n_rel:] = low
    blocks, width, per = query.shape
    half = width // 2
    ones = jnp.ones((ids.shape[2], 128), BF)
    for b in range(blocks):
        lst, span = b // 2, b % 2
        lanes = slice(span * per, (span + 1) * per)
        left = dot_nn(table[...], one_hot(ids[lst, LHS : LHS + 1, lanes], table.shape[1]))
        hot_rel = one_hot(ids[lst, REL : REL + 1, lanes], n_rel)
        rel_col = dot_nn(rel_parts[:, :n_rel], hot_rel) + dot_nn(rel_parts[:, n_rel:], hot_rel)
        rel_cols[b] = rel_col
        l_re, l_im = left[:half], left[half:]
        r_re, r_im = rel_col[:half], rel_col[half:]
        query[b, :half] = (l_re * r_re - l_im * r_im).astype(BF)
        query[b, half:] = (l_re * r_im + l_im * r_re).astype(BF)
        counts[b] = dot_nn(one_hot(ids[lst, NEG + span : NEG + span + 1, :], rows), ones)


def grad_kernel(n_negs, ids, query, rel_cols, counts, far, keep, send, near, far_grad):
    blocks, width, per = query.shape
    half = width // 2
    rows = far.shape[1]
    table_rows = near.shape[1]
    far_t = far[...].astype(F32).T.astype(BF)
    for b in range(blocks):
        lst, span = b // 2, b % 2
        lanes = slice(span * per, (span + 1) * per)
        q = query[b]
        scores = dot_nn(far_t, q)
        row_ids = lax.broadcasted_iota(jnp.int32, (rows, per), 0)
        right = row_ids == ids[lst, RHS : RHS + 1, lanes]
        place = lax.broadcasted_iota(jnp.int32, (1, per), 1) + span * per
        mask = jnp.where(place < ids[lst, LIVE : LIVE + 1, lanes], 1.0, 0.0)
        positive = jnp.sum(jnp.where(right, scores, 0.0), axis=0, keepdims=True)
        grad_pos = -jax.nn.sigmoid(-positive) * mask
        grad_neg = (jax.nn.sigmoid(scores) * (mask / n_negs)).astype(BF).astype(F32)
        times = jnp.concatenate([counts[b]] * (per // 128), axis=1)
        grad = grad_neg * times + jnp.where(right, grad_pos, 0.0)
        high, low = split(grad)
        add_far = dot_nt(q, high) + dot_nt(q, low)
        gq = dot_nn(far[...], high) + dot_nn(far[...], low)
        r_re, r_im = rel_cols[b, :half], rel_cols[b, half:]
        g_re, g_im = gq[:half], gq[half:]
        left = jnp.concatenate([g_re * r_re + g_im * r_im, g_im * r_re - g_re * r_im], axis=0)
        left_hot = one_hot(ids[lst, LHS : LHS + 1, lanes], table_rows)
        high, low = split(left)
        add_near = dot_nt(high, left_hot) + dot_nt(low, left_hot)
        if b == 0:
            far_grad[...] = add_far
            near[...] = add_near
        else:
            far_grad[...] += add_far
            near[...] += add_near
    core = lax.axis_index("rep") % 2
    cut = rows // 2
    mine, theirs = (pl.ds(pl.multiple_of(c * cut, cut), cut) for c in (core, 1 - core))
    hot_mine, hot_theirs = (
        pl.ds(pl.multiple_of(rows + c * cut, cut), cut) for c in (core, 1 - core)
    )
    keep[:, :cut] = near[:, mine]
    keep[:, cut : 2 * cut] = near[:, hot_mine]
    keep[:, 2 * cut :] = far_grad[:, mine]
    send[:, :cut] = near[:, theirs].astype(BF)
    send[:, cut : 2 * cut] = near[:, hot_theirs].astype(BF)
    send[:, 2 * cut :] = far_grad[:, theirs].astype(BF)


def pair_kernel(keep, got, own, hot, far_hot):
    cut = own.shape[1]
    total = keep[...] + got[...].astype(F32)
    own[...] = total[:, :cut]
    hot_bf = total[:, cut : 2 * cut].astype(BF)
    hot[...] = hot_bf
    far_hot[:, cut:] = hot_bf
    far_hot[:, :cut] = total[:, 2 * cut :].astype(BF)


def whole_kernel(shift, own, hot, far_hot, *rest):
    *others, out = rest
    cut = own.shape[1]
    out[:, :cut] = (own[...] + far_hot[:, :cut].astype(F32)).astype(BF)
    parts = {0: hot[...], shift: far_hot[:, cut:]}
    for distance, ref in zip([k for k in (1, 2, 3) if k != shift], others, strict=True):
        parts[distance] = ref[...]
    parts = {k: v.astype(F32) for k, v in parts.items()}
    out[:, cut:] = ((parts[0] + parts[2]) + (parts[1] + parts[3])).astype(BF)


def update_kernel(mine, got, emb, acc, hot, hot_acc, new_emb, new_acc, new_hot, new_hot_acc):
    core = lax.axis_index("rep") % 2
    cut = mine.shape[1] // 2
    width = mine.shape[0]
    for ref, c in ((mine, core), (got, 1 - core)):
        lanes = pl.ds(pl.multiple_of(c * cut, cut), cut)
        for start, w, a, new_w, new_a in (
            (0, emb, acc, new_emb, new_acc),
            (cut, hot, hot_acc, new_hot, new_hot_acc),
        ):
            grad = ref[:, start : start + cut].astype(F32)
            accum = a[:, lanes] + jnp.sum(grad * grad, axis=0, keepdims=True) / width
            new_a[:, lanes] = accum
            new_w[:, lanes] = w[:, lanes] - LEARN_RATE * grad / jnp.sqrt(accum)


def shifted(block, axis, distance):
    size = lax.axis_size(axis)
    return lax.ppermute(block, axis, [((i - distance) % size, i) for i in range(size)])


def swapped(block, bit):
    return lax.ppermute(block, "rep", [(i, i ^ bit) for i in range(lax.axis_size("rep"))])


def struct(shape, dtype):
    return jax.ShapeDtypeStruct(shape, dtype)


def bucket(fetch, home, operands):
    count, lhs, rhs, rel_ids, neg, emb, acc, hot, hot_acc, rel = operands
    width, rows = emb.shape
    table_rows = rows + hot.shape[1]
    edges = lhs.shape[1]
    spans, n_negs = neg.shape[1:]
    per = edges // spans
    blocks = 2 * spans
    emb_bf, ids = call(
        pack_kernel,
        (struct((width, rows), BF), struct((8, edges), jnp.int32)),
        smem=(0,),
        n_in=6,
    )(count, emb, lhs, rhs, rel_ids, neg)
    far = fetch(emb_bf)
    other = swapped(ids, 2)
    all_ids, query, rel_cols, counts = call(
        query_kernel,
        (
            struct((2, 8, edges), jnp.int32),
            struct((blocks, width, per), BF),
            struct((blocks, width, per), F32),
            struct((blocks, rows, 128), F32),
        ),
        scratch=[pltpu.VMEM((width, table_rows), BF), pltpu.VMEM((width, 2 * rel.shape[1]), BF)],
        n_in=5,
        flops=6 * blocks * per * width * table_rows,
        nbytes=8_000_000,
    )(ids, other, emb, hot, rel)
    cut = rows // 2
    keep, send = call(
        functools.partial(grad_kernel, n_negs),
        (struct((width, 3 * cut), F32), struct((width, 3 * cut), BF)),
        scratch=[pltpu.VMEM((width, table_rows), F32), pltpu.VMEM((width, rows), F32)],
        n_in=5,
        flops=6 * blocks * per * width * table_rows,
        nbytes=8_000_000,
    )(all_ids, query, rel_cols, counts, far)
    got = swapped(send, 1)
    own, hot_part, far_hot = call(
        pair_kernel,
        (struct((width, cut), F32), struct((width, cut), BF), struct((width, 2 * cut), BF)),
        n_in=2,
    )(keep, got)
    mine = home(own, hot_part, far_hot)
    theirs = swapped(mine, 1)
    return call(
        update_kernel,
        (
            struct(emb.shape, F32),
            struct(acc.shape, F32),
            struct(hot.shape, F32),
            struct(hot_acc.shape, F32),
        ),
        n_in=6,
    )(mine, theirs, emb, acc, hot, hot_acc)


def home_by(shift, own, hot, far_hot):
    arrived = shifted(far_hot, "dom", shift)
    others = [shifted(hot, "dom", k) for k in (1, 2, 3) if k != shift]
    return call(
        functools.partial(whole_kernel, shift),
        struct(far_hot.shape, BF),
        n_in=3 + len(others),
    )(own, hot, arrived, *others)


def four_workers(offset, operands):
    def branch(shift):
        return lambda *args: tuple(
            bucket(
                lambda block: shifted(block, "dom", -shift),
                functools.partial(home_by, shift),
                args,
            )
        )

    return lax.switch(offset - 1, [branch(1), branch(2), branch(3)], *operands)


def digit_set(offset, digit):
    return offset // (1 << digit) % 2 == 1


def many_workers(offset, operands):
    digits = lax.axis_size("dom").bit_length() - 1

    def moved(block, sign):
        for digit in range(digits):
            block = jnp.where(
                digit_set(offset, digit), shifted(block, "dom", sign * (1 << digit)), block
            )
        return block

    def home(own, hot, far_hot):
        cut = own.shape[1]
        arrived = moved(far_hot[:, :cut], 1)
        total = hot
        for digit in range(digits):
            size = lax.axis_size("dom")
            route = [(i, i ^ (1 << digit)) for i in range(size)]
            total = (total.astype(F32) + lax.ppermute(total, "dom", route).astype(F32)).astype(BF)
        return jnp.concatenate([(own + arrived.astype(F32)).astype(BF), total], axis=1)

    return bucket(lambda block: moved(block, -1), home, operands)


def body(
    plan, edge_lhs, edge_rhs, edge_rel, edge_count, negatives, emb, acc, hot_emb, hot_acc, relations
):
    workers = lax.axis_size("dom")
    offset = (plan[0] - lax.axis_index("dom")) % workers
    operands = (
        edge_count,
        edge_lhs,
        edge_rhs,
        edge_rel,
        negatives,
        emb.T,
        acc[None, :],
        hot_emb.T,
        hot_acc[None, :],
        relations.T,
    )
    run = four_workers if workers == 4 else many_workers
    new_emb, new_acc, new_hot, new_hot_acc = run(offset, operands)
    return (new_emb.T, new_acc[0], new_hot.T, new_hot_acc[0])


def solution(mesh):
    placed = (
        P("dom"),
        P(("groups", "dom"), "rep"),
        P(("groups", "dom"), "rep"),
        P(("groups", "dom"), "rep"),
        P(("groups", "dom", "rep")),
        P(("groups", "dom"), "rep", None),
        P(("groups", "dom"), None),
        P(("groups", "dom")),
        P("groups", None),
        P("groups"),
        P("groups", None),
    )
    return jax.shard_map(
        body,
        mesh=mesh,
        in_specs=placed,
        out_specs=(
            P(("groups", "dom"), None),
            P(("groups", "dom")),
            P("groups", None),
            P("groups"),
        ),
        check_vma=False,
    )
```

```python
import functools

import jax
import jax.numpy as jnp
from jax import lax
from jax.experimental import pallas as pl
from jax.experimental.pallas import tpu as pltpu
from jax.sharding import PartitionSpec as P

LEARN_RATE = 0.5
TWO = {1: True, 2: True, 3: True}
BF = jnp.bfloat16
F32 = jnp.float32
LHS, RHS, REL, NEG, LIVE = 0, 1, 2, 3, 5
VMEM_LIMIT = 24 * 1024 * 1024


def call(kernel, out_shape, n_in, scratch=(), anywhere=(), limit=VMEM_LIMIT):
    specs = [
        pl.BlockSpec(memory_space=pl.ANY if i in anywhere else pltpu.VMEM) for i in range(n_in)
    ]
    return pl.pallas_call(
        kernel,
        out_shape=out_shape,
        in_specs=specs,
        scratch_shapes=list(scratch),
        compiler_params=pltpu.CompilerParams(vmem_limit_bytes=limit),
        cost_estimate=pl.CostEstimate(flops=1, bytes_accessed=1, transcendentals=0),
    )


def split(x):
    high = x.astype(BF)
    return high, (x - high.astype(F32)).astype(BF)


def dot_nt(a, b):
    return lax.dot_general(a, b, (((1,), (1,)), ((), ())), preferred_element_type=F32)


def dot_nn(a, b):
    return jnp.dot(a, b, preferred_element_type=F32)


def one_hot(ids, count):
    rows = lax.broadcasted_iota(jnp.int32, (count, ids.shape[1]), 0)
    return jnp.where(rows == ids, 1.0, 0.0).astype(BF)


def halves(axis_size):
    core = lax.axis_index("rep") % 2
    cut = axis_size // 2
    return [pl.ds(pl.multiple_of(c * cut, cut), cut) for c in (core, 1 - core)]


def pack_kernel(plan, count, emb, lhs, rhs, rel, neg, half, ids, offset):
    workers = lax.axis_size("dom")
    offset[...] = lax.rem(plan[0] - lax.axis_index("dom") + workers, workers)
    half[...] = emb[:, halves(emb.shape[1])[0]].astype(BF)
    width = ids.shape[1]
    ids[...] = jnp.full(ids.shape, -1, jnp.int32)
    ids[LHS : LHS + 1, :] = lhs[...]
    ids[RHS : RHS + 1, :] = rhs[...]
    ids[REL : REL + 1, :] = rel[...]
    ids[NEG : NEG + 2, 0 : neg.shape[2]] = neg[0]
    ids[LIVE : LIVE + 1, :] = jnp.broadcast_to(count[...], (1, width))


def tables_kernel(emb, hot, rel, table, rel_parts):
    rows = emb.shape[1]
    n_rel = rel.shape[1]
    table[:, :rows] = emb[...].astype(BF)
    table[:, rows:] = hot[...].astype(BF)
    high, low = split(rel[...])
    rel_parts[:, :n_rel] = high
    rel_parts[:, n_rel:] = low


def list_columns(ids, table, rel_parts, query, rel_cols, counts):
    n_rel = rel_parts.shape[1] // 2
    rows = counts.shape[1]
    spans, width, per = query.shape
    half = width // 2
    for b in range(spans):
        lanes = slice(b * per, (b + 1) * per)
        left = dot_nn(table[...], one_hot(ids[LHS : LHS + 1, lanes], table.shape[1]))
        hot_rel = one_hot(ids[REL : REL + 1, lanes], n_rel)
        rel_col = dot_nn(rel_parts[:, :n_rel], hot_rel) + dot_nn(rel_parts[:, n_rel:], hot_rel)
        rel_cols[b] = rel_col
        l_re, l_im = left[:half], left[half:]
        r_re, r_im = rel_col[:half], rel_col[half:]
        query[b, :half] = (l_re * r_re - l_im * r_im).astype(BF)
        query[b, half:] = (l_re * r_im + l_im * r_re).astype(BF)
        named = ids[NEG + b : NEG + b + 1, :]
        row_ids = lax.broadcasted_iota(jnp.int32, (rows, 128), 0)
        times = jnp.zeros((rows, 128), F32)
        for start in range(0, named.shape[1], 128):
            times += jnp.where(row_ids == named[:, start : start + 128], 1.0, 0.0)
        counts[b] = jnp.broadcast_to(jnp.sum(times, axis=1, keepdims=True), times.shape)


def first_kernel(emb, hot, rel, ids, table, rel_parts, query, rel_cols, counts):
    tables_kernel(emb, hot, rel, table, rel_parts)
    list_columns(ids, table, rel_parts, query, rel_cols, counts)


def relay_kernel(one, after, other, out):
    del after, other
    out[...] = one[...]


def second_kernel(table, rel_parts, ids, query, rel_cols, counts):
    list_columns(ids, table, rel_parts, query, rel_cols, counts)


def hot_kernel(n_negs, far_half, far_rest, *refs):
    lists = (refs[0:4], refs[4:8])
    grads, lefts, keep, send, *totals, far = refs[8:]
    mine, theirs = halves(far.shape[1])
    far[:, mine] = far_half[...]
    far[:, theirs] = far_rest[...]
    rows = far.shape[1]
    hot_rows = totals[0].shape[1]
    far_t = far[...].astype(F32).T.astype(BF)
    for i, (ids, query, rel_cols, counts) in enumerate(lists):
        spans, width, per = query.shape
        half = width // 2
        for b in range(spans):
            lanes = slice(b * per, (b + 1) * per)
            scores = dot_nn(far_t, query[b])
            row_ids = lax.broadcasted_iota(jnp.int32, (rows, per), 0)
            right = row_ids == ids[RHS : RHS + 1, lanes]
            place = lax.broadcasted_iota(jnp.int32, (1, per), 1) + b * per
            mask = jnp.where(place < ids[LIVE : LIVE + 1, lanes], 1.0, 0.0)
            positive = jnp.sum(jnp.where(right, scores, 0.0), axis=0, keepdims=True)
            grad_pos = -jax.nn.sigmoid(-positive) * mask
            times = jnp.concatenate([counts[b]] * (per // 128), axis=1)
            grad = (jax.nn.sigmoid(scores) * (mask / n_negs)).astype(BF).astype(F32) * times
            grad = (grad + jnp.where(right, grad_pos, 0.0)).astype(BF)
            grads[i * spans + b] = grad
            gq = dot_nn(far[...], grad)
            r_re, r_im = rel_cols[b, :half], rel_cols[b, half:]
            g_re, g_im = gq[:half], gq[half:]
            lefts[i * spans + b, :half] = (g_re * r_re + g_im * r_im).astype(BF)
            lefts[i * spans + b, half:] = (g_im * r_re - g_re * r_im).astype(BF)
            left_hot = one_hot(ids[LHS : LHS + 1, lanes] - rows, hot_rows)
            add = dot_nt(lefts[i * spans + b], left_hot)
            if b == 0:
                totals[i][...] = add
            else:
                totals[i][...] += add
    mine, theirs = halves(hot_rows)
    keep[...] = totals[0][:, mine] + totals[1][:, mine]
    send[...] = (totals[0][:, theirs] + totals[1][:, theirs]).astype(BF)


def parts_kernel(ids_0, ids_1, query_0, query_1, grads, lefts, after, keep, send, *totals):
    del after
    rows = totals[0].shape[1]
    for i, (ids, query) in enumerate(((ids_0, query_0), (ids_1, query_1))):
        own, far_grad = totals[2 * i : 2 * i + 2]
        spans, width, per = query.shape
        for b in range(spans):
            lanes = slice(b * per, (b + 1) * per)
            add_far = dot_nt(query[b], grads[i * spans + b])
            add_own = dot_nt(lefts[i * spans + b], one_hot(ids[LHS : LHS + 1, lanes], rows))
            if b == 0:
                far_grad[...] = add_far
                own[...] = add_own
            else:
                far_grad[...] += add_far
                own[...] += add_own
    mine, theirs = halves(rows)
    cut = rows // 2
    for j in range(2):
        lanes = slice(j * cut, (j + 1) * cut)
        keep[:, lanes] = totals[j][:, mine] + totals[2 + j][:, mine]
        send[:, lanes] = (totals[j][:, theirs] + totals[2 + j][:, theirs]).astype(BF)


def hot_pair_kernel(keep, got, hot):
    hot[...] = (keep[...] + got[...].astype(F32)).astype(BF)


def parts_pair_kernel(keep, got, own, far):
    cut = own.shape[1]
    total = keep[...] + got[...].astype(F32)
    own[...] = total[:, :cut]
    far[...] = total[:, cut:].astype(BF)


def add_kernel(one, other, out):
    out[...] = (one[...].astype(F32) + other[...].astype(F32)).astype(BF)


def own_kernel(own, far, out):
    out[...] = own[...] + far[...].astype(F32)


def whole_kernel(own, *refs):
    *hot, out = refs
    cut = own.shape[1]
    out[:, :cut] = own[...]
    pairs = [
        hot[i][...].astype(F32) + hot[i + 1][...].astype(F32) for i in range(0, len(hot), 2)
    ]
    out[:, cut:] = sum(pairs[1:], pairs[0])


def adagrad(weights, accum, grad):
    new = accum + jnp.sum(grad * grad, axis=0, keepdims=True) / grad.shape[0]
    return weights - LEARN_RATE * grad / jnp.sqrt(new), new


def near_update_kernel(grads, emb, acc, hot, hot_acc, done, done_acc, rest, rest_acc):
    cut = grads.shape[1] // 2
    mine, theirs = halves(2 * cut)
    for i, (w, a) in enumerate(((emb, acc), (hot, hot_acc))):
        lanes = slice(i * cut, (i + 1) * cut)
        done[:, lanes], done_acc[:, lanes] = adagrad(w[:, mine], a[:, mine], grads[:, lanes])
        rest[:, lanes] = w[:, theirs]
        rest_acc[:, lanes] = a[:, theirs]


def far_update_kernel(grads, done, done_acc, rest, rest_acc, emb, acc, hot, hot_acc):
    cut = grads.shape[1] // 2
    mine, theirs = halves(2 * cut)
    for i, (w, a) in enumerate(((emb, acc), (hot, hot_acc))):
        lanes = slice(i * cut, (i + 1) * cut)
        w[:, mine] = done[:, lanes]
        a[:, mine] = done_acc[:, lanes]
        w[:, theirs], a[:, theirs] = adagrad(rest[:, lanes], rest_acc[:, lanes], grads[:, lanes])


def shifted(block, axis, distance):
    size = lax.axis_size(axis)
    return lax.ppermute(block, axis, [((i - distance) % size, i) for i in range(size)])


def swapped(block, bit):
    return lax.ppermute(block, "rep", [(i, i ^ bit) for i in range(lax.axis_size("rep"))])


def struct(shape, dtype):
    return jax.ShapeDtypeStruct(shape, dtype)


def bucket(fetch, home, hot_sum, emb_half, ids, emb, hot, rel, n_negs, spans):
    width, rows = emb.shape
    hot_rows = hot.shape[1]
    edges = ids.shape[1]
    per = edges // spans
    blocks = 2 * spans
    far_half = fetch(emb_half)
    other = swapped(ids, 2)
    columns = (
        struct((spans, width, per), BF),
        struct((spans, width, per), F32),
        struct((spans, rows, 128), F32),
    )
    table, rel_parts, *mine = call(
        first_kernel,
        (struct((width, rows + hot_rows), BF), struct((width, 2 * rel.shape[1]), BF), *columns),
        n_in=4,
    )(emb, hot, rel, ids)
    far_half = call(relay_kernel, struct(far_half.shape, BF), n_in=3, anywhere=(1, 2))(
        far_half, table, other
    )
    far_rest = swapped(far_half, 1)
    theirs = call(second_kernel, columns, n_in=3)(table, rel_parts, other)
    cut = rows // 2
    grads, lefts, hot_keep, hot_send = call(
        functools.partial(hot_kernel, n_negs),
        (
            struct((blocks, rows, per), BF),
            struct((blocks, width, per), BF),
            struct((width, hot_rows // 2), F32),
            struct((width, hot_rows // 2), BF),
        ),
        scratch=[pltpu.VMEM((width, hot_rows), F32)] * 2 + [pltpu.VMEM((width, rows), BF)],
        n_in=10,
    )(far_half, far_rest, ids, *mine, other, *theirs)
    hot_got = swapped(hot_send, 1)
    hot_half = call(hot_pair_kernel, struct(hot_send.shape, BF), n_in=2)(hot_keep, hot_got)
    keep, send = call(
        parts_kernel,
        (struct((width, 2 * cut), F32), struct((width, 2 * cut), BF)),
        scratch=[pltpu.VMEM((width, rows), F32)] * 4,
        n_in=7,
        anywhere=(6,),
    )(ids, other, mine[0], theirs[0], grads, lefts, hot_half)
    got = swapped(send, 1)
    hot_parts = hot_sum(hot_half)
    own, far_half = call(
        parts_pair_kernel,
        (struct((width, cut), F32), struct((width, cut), BF)),
        n_in=2,
    )(keep, got)
    own = call(own_kernel, struct(own.shape, F32), n_in=2)(own, home(far_half))
    hot_refs = [ref for pair in hot_parts for ref in pair]
    return call(whole_kernel, struct((width, cut + hot_rows // 2), F32), n_in=1 + len(hot_refs))(
        own, *hot_refs
    )


def direct_sum(hot):
    h1, h2, h3 = (shifted(hot, "dom", k) for k in (1, 2, 3))
    return ((hot, h2), (h1, h3))


def doubled_sum(hot):
    size = lax.axis_size("dom")
    digits = size.bit_length() - 1
    for digit in range(digits):
        route = [(i, i ^ (1 << digit)) for i in range(size)]
        other = lax.ppermute(hot, "dom", route)
        if digit == digits - 1:
            return ((hot, other),)
        hot = call(add_kernel, struct(hot.shape, BF), n_in=2)(hot, other)


def four_workers(offset, arrays, sizes):
    def branch(shift):
        def run(*arrays):
            return bucket(
                lambda block: shifted(block, "dom", -shift),
                lambda block: shifted(block, "dom", shift),
                doubled_sum if TWO[shift] else direct_sum,
                *arrays,
                *sizes,
            )

        return run

    return lax.switch(offset - 1, [branch(1), branch(2), branch(3)], *arrays)


def digit_set(offset, digit):
    return offset // (1 << digit) % 2 == 1


def many_workers(offset, arrays, sizes):
    size = lax.axis_size("dom")
    digits = size.bit_length() - 1

    def moved(block, sign):
        for digit in range(digits):
            block = jnp.where(
                digit_set(offset, digit), shifted(block, "dom", sign * (1 << digit)), block
            )
        return block

    return bucket(
        lambda block: moved(block, -1), lambda block: moved(block, 1), doubled_sum, *arrays, *sizes
    )


def body(
    plan, edge_lhs, edge_rhs, edge_rel, edge_count, negatives, emb, acc, hot_emb, hot_acc, relations
):
    emb, acc, hot, hot_acc, rel = emb.T, acc[None, :], hot_emb.T, hot_acc[None, :], relations.T
    edges = edge_lhs.shape[1]
    spans, n_negs = negatives.shape[1:]
    emb_half, ids, offset = call(
        pack_kernel,
        (
            struct((emb.shape[0], emb.shape[1] // 2), BF),
            struct((8, edges), jnp.int32),
            struct((1,), jnp.int32),
        ),
        n_in=7,
        limit=60 * 1024 * 1024,
    )(plan[None, :], edge_count[None, :], emb, edge_lhs, edge_rhs, edge_rel, negatives)
    run = four_workers if lax.axis_size("dom") == 4 else many_workers
    mine = run(offset[0], (emb_half, ids, emb, hot, rel), (n_negs, spans))
    theirs = swapped(mine, 1)
    half, half_acc = struct(mine.shape, F32), struct((1, mine.shape[1]), F32)
    ready = call(near_update_kernel, (half, half_acc, half, half_acc), n_in=5)(
        mine, emb, acc, hot, hot_acc
    )
    new_emb, new_acc, new_hot, new_hot_acc = call(
        far_update_kernel, tuple(struct(x.shape, F32) for x in (emb, acc, hot, hot_acc)), n_in=5
    )(theirs, *ready)
    return (new_emb.T, new_acc[0], new_hot.T, new_hot_acc[0])


def solution(mesh):
    placed = (
        P("dom"),
        P(("groups", "dom"), "rep"),
        P(("groups", "dom"), "rep"),
        P(("groups", "dom"), "rep"),
        P(("groups", "dom", "rep")),
        P(("groups", "dom"), "rep", None),
        P(("groups", "dom"), None),
        P(("groups", "dom")),
        P("groups", None),
        P("groups"),
        P("groups", None),
    )
    return jax.shard_map(
        body,
        mesh=mesh,
        in_specs=placed,
        out_specs=(
            P(("groups", "dom"), None),
            P(("groups", "dom")),
            P("groups", None),
            P("groups"),
        ),
        check_vma=False,
    )
```

```python
import functools

import jax
import jax.numpy as jnp
from jax import lax
from jax.experimental import pallas as pl
from jax.experimental.pallas import tpu as pltpu
from jax.sharding import PartitionSpec as P

LEARN_RATE = 0.5
BF = jnp.bfloat16
F32 = jnp.float32
LHS, RHS, REL, NEG, LIVE = 0, 1, 2, 3, 5
VMEM_LIMIT = 24 * 1024 * 1024


def call(kernel, out_shape, n_in, scratch=(), anywhere=(), smem=()):
    spaces = [
        pltpu.SMEM if i in smem else pl.ANY if i in anywhere else pltpu.VMEM for i in range(n_in)
    ]
    return pl.pallas_call(
        kernel,
        out_shape=out_shape,
        in_specs=[pl.BlockSpec(memory_space=space) for space in spaces],
        scratch_shapes=list(scratch),
        compiler_params=pltpu.CompilerParams(vmem_limit_bytes=VMEM_LIMIT),
        cost_estimate=pl.CostEstimate(flops=1, bytes_accessed=1, transcendentals=0),
    )


def dot_nt(a, b):
    return lax.dot_general(a, b, (((1,), (1,)), ((), ())), preferred_element_type=F32)


def dot_nn(a, b):
    return jnp.dot(a, b, preferred_element_type=F32)


def one_hot(ids, count):
    rows = lax.broadcasted_iota(jnp.int32, (count, ids.shape[1]), 0).astype(jnp.int16)
    return jnp.where(rows == ids.astype(jnp.int16), jnp.ones((), BF), jnp.zeros((), BF))


def fetch_all(pairs, sems):
    copies = [
        pltpu.make_async_copy(src, dst, sems.at[i]) for i, (src, dst) in enumerate(pairs)
    ]
    for copy in copies:
        copy.start()
    return copies


def halves(axis_size):
    core = lax.axis_index("rep") % 2
    cut = axis_size // 2
    return [pl.ds(pl.multiple_of(c * cut, cut), cut) for c in (core, 1 - core)]


def pack_kernel(count, emb, lhs, rhs, rel, neg, half, ids):
    half[...] = emb[:, halves(emb.shape[1])[0]].astype(BF)
    width = ids.shape[1]
    ids[...] = jnp.full(ids.shape, -1, jnp.int32)
    ids[LHS : LHS + 1, :] = lhs[...]
    ids[RHS : RHS + 1, :] = rhs[...]
    ids[REL : REL + 1, :] = rel[...]
    ids[NEG : NEG + 2, 0 : neg.shape[2]] = neg[0]
    ids[LIVE : LIVE + 1, :] = jnp.full((1, width), count[0], jnp.int32)


def count_rows(ids, counts):
    spans, rows, _ = counts.shape
    for b in range(spans):
        named = ids[NEG + b : NEG + b + 1, :]
        row_ids = lax.broadcasted_iota(jnp.int32, (rows, 128), 0)
        times = jnp.zeros((rows, 128), F32)
        for start in range(0, named.shape[1], 128):
            times += jnp.where(row_ids == named[:, start : start + 128], 1.0, 0.0)
        counts[b] = jnp.broadcast_to(jnp.sum(times, axis=1, keepdims=True), times.shape)


def list_columns(ids, table, rel_parts, query, rel_cols):
    spans, width, per = query.shape
    half = width // 2
    n_rel = rel_parts.shape[1] // 2
    for b in range(spans):
        lanes = slice(b * per, (b + 1) * per)
        left = dot_nn(table[...], one_hot(ids[LHS : LHS + 1, lanes], table.shape[1]))
        rel_hot = one_hot(ids[REL : REL + 1, lanes], n_rel)
        rel_col = dot_nn(rel_parts[:, :n_rel], rel_hot) + dot_nn(rel_parts[:, n_rel:], rel_hot)
        rel_cols[b] = rel_col
        l_re, l_im = left[:half], left[half:]
        r_re, r_im = rel_col[:half], rel_col[half:]
        query[b, :half] = (l_re * r_re - l_im * r_im).astype(BF)
        query[b, half:] = (l_re * r_im + l_im * r_re).astype(BF)


def first_kernel(
    emb, hot, rel, ids, table, rel_parts, query, rel_cols, counts, emb_s, hot_s, rel_s, sems
):
    copies = fetch_all([(emb, emb_s), (hot, hot_s), (rel, rel_s)], sems)
    count_rows(ids, counts)
    rows = emb.shape[1]
    copies[0].wait()
    table[:, :rows] = emb_s[...].astype(BF)
    copies[1].wait()
    table[:, rows:] = hot_s[...].astype(BF)
    copies[2].wait()
    n_rel = rel.shape[1]
    high = rel_s[...].astype(BF)
    rel_parts[:, :n_rel] = high
    rel_parts[:, n_rel:] = (rel_s[...] - high.astype(F32)).astype(BF)
    list_columns(ids, table, rel_parts, query, rel_cols)


def second_kernel(table, rel_parts, ids, query, rel_cols, counts):
    count_rows(ids, counts)
    list_columns(ids, table, rel_parts, query, rel_cols)


def relay_kernel(one, after, other, out):
    del after, other
    out[...] = one[...]


def edges_kernel(n_negs, far_half, far_rest, *refs):
    lists = (refs[0:4], refs[4:8])
    lefts, keep, send, far, *totals = refs[8:]
    mine, theirs = halves(far.shape[1])
    far[:, mine] = far_half[...]
    far[:, theirs] = far_rest[...]
    rows = far.shape[1]
    hot_rows = totals[0].shape[1]
    far_t = far[...].astype(F32).T.astype(BF)
    for i, (ids, query, rel_cols, counts) in enumerate(lists):
        hot_total, far_total = totals[2 * i : 2 * i + 2]
        spans, width, per = query.shape
        half = width // 2
        for b in range(spans):
            at = i * spans + b
            lanes = slice(b * per, (b + 1) * per)
            scores = dot_nn(far_t, query[b])
            row_ids = lax.broadcasted_iota(jnp.int32, (rows, per), 0)
            right = row_ids == ids[RHS : RHS + 1, lanes]
            place = lax.broadcasted_iota(jnp.int32, (1, per), 1) + b * per
            mask = jnp.where(place < ids[LIVE : LIVE + 1, lanes], 1.0, 0.0)
            chance = 0.5 * jnp.tanh(0.5 * scores) + 0.5
            times = jnp.concatenate([counts[b]] * (per // 128), axis=1)
            grad = (chance * (mask / n_negs)).astype(BF).astype(F32) * times
            grad = (grad + jnp.where(right, (chance - 1.0) * mask, 0.0)).astype(BF)
            gq = dot_nn(far[...], grad)
            r_re, r_im = rel_cols[b, :half], rel_cols[b, half:]
            g_re, g_im = gq[:half], gq[half:]
            lefts[at, :half] = (g_re * r_re + g_im * r_im).astype(BF)
            lefts[at, half:] = (g_im * r_re - g_re * r_im).astype(BF)
            left_hot = one_hot(ids[LHS : LHS + 1, lanes] - rows, hot_rows)
            add_hot = dot_nt(lefts[at], left_hot)
            add_far = dot_nt(query[b], grad)
            if b == 0:
                hot_total[...] = add_hot
                far_total[...] = add_far
            else:
                hot_total[...] += add_hot
                far_total[...] += add_far
    cut = hot_rows // 2
    for j, (mine, theirs) in enumerate((halves(hot_rows), halves(rows))):
        lanes = slice(0, cut) if j == 0 else slice(cut, cut + rows // 2)
        keep[:, lanes] = totals[j][:, mine] + totals[2 + j][:, mine]
        send[:, lanes] = (totals[j][:, theirs] + totals[2 + j][:, theirs]).astype(BF)


def own_kernel(ids_0, ids_1, lefts, after, keep, send, *totals):
    del after
    per = lefts.shape[2]
    rows = totals[0].shape[1]
    for i, ids in enumerate((ids_0, ids_1)):
        spans = lefts.shape[0] // 2
        for b in range(spans):
            left_own = one_hot(ids[LHS : LHS + 1, b * per : (b + 1) * per], rows)
            add = dot_nt(lefts[i * spans + b], left_own)
            if b == 0:
                totals[i][...] = add
            else:
                totals[i][...] += add
    mine, theirs = halves(rows)
    keep[...] = totals[0][:, mine] + totals[1][:, mine]
    send[...] = (totals[0][:, theirs] + totals[1][:, theirs]).astype(BF)


def pair_kernel(keep, got, hot, far):
    total = (keep[...] + got[...].astype(F32)).astype(BF)
    cut = hot.shape[1]
    hot[...] = total[:, :cut]
    far[...] = total[:, cut:]


def add_kernel(one, other, out):
    out[...] = (one[...].astype(F32) + other[...].astype(F32)).astype(BF)


def own_sum_kernel(keep, got, far, out):
    out[...] = (keep[...] + got[...].astype(F32)) + far[...].astype(F32)


def whole_kernel(own, one, other, out):
    cut = own.shape[1]
    out[:, :cut] = own[...]
    out[:, cut:] = one[...].astype(F32) + other[...].astype(F32)


def adagrad(weights, accum, grad):
    new = accum + jnp.sum(grad * grad, axis=0, keepdims=True) / grad.shape[0]
    return weights - LEARN_RATE * grad / jnp.sqrt(new), new


def near_update_kernel(grads, emb, acc, hot, hot_acc, done, done_acc, rest, rest_acc):
    cut = grads.shape[1] // 2
    mine, theirs = halves(2 * cut)
    for i, (w, a) in enumerate(((emb, acc), (hot, hot_acc))):
        lanes = slice(i * cut, (i + 1) * cut)
        done[:, lanes], done_acc[:, lanes] = adagrad(w[:, mine], a[:, mine], grads[:, lanes])
        rest[:, lanes] = w[:, theirs]
        rest_acc[:, lanes] = a[:, theirs]


def far_update_kernel(grads, done, done_acc, rest, rest_acc, emb, acc, hot, hot_acc):
    cut = grads.shape[1] // 2
    mine, theirs = halves(2 * cut)
    for i, (w, a) in enumerate(((emb, acc), (hot, hot_acc))):
        lanes = slice(i * cut, (i + 1) * cut)
        w[:, mine] = done[:, lanes]
        a[:, mine] = done_acc[:, lanes]
        w[:, theirs], a[:, theirs] = adagrad(rest[:, lanes], rest_acc[:, lanes], grads[:, lanes])


def shifted(block, axis, distance):
    size = lax.axis_size(axis)
    return lax.ppermute(block, axis, [((i - distance) % size, i) for i in range(size)])


def swapped(block, bit):
    return lax.ppermute(block, "rep", [(i, i ^ bit) for i in range(lax.axis_size("rep"))])


def struct(shape, dtype):
    return jax.ShapeDtypeStruct(shape, dtype)


def bucket(fetch, home, count, lhs, rhs, rel_ids, neg, emb, hot, rel):
    width, rows = emb.shape
    hot_rows = hot.shape[1]
    edges = lhs.shape[1]
    spans, n_negs = neg.shape[1:]
    per = edges // spans
    blocks = 2 * spans
    emb_half, ids = call(
        pack_kernel,
        (struct((width, rows // 2), BF), struct((8, edges), jnp.int32)),
        n_in=6,
        smem=(0,),
    )(count, emb, lhs, rhs, rel_ids, neg)
    far_half = fetch(emb_half)
    other = swapped(ids, 2)
    columns = (
        struct((spans, width, per), BF),
        struct((spans, width, per), F32),
        struct((spans, rows, 128), F32),
    )
    table, rel_parts, *mine = call(
        first_kernel,
        (struct((width, rows + hot_rows), BF), struct((width, 2 * rel.shape[1]), BF), *columns),
        n_in=4,
        anywhere=(0, 1, 2),
        scratch=[pltpu.VMEM(x.shape, F32) for x in (emb, hot, rel)] + [pltpu.SemaphoreType.DMA((3,))],
    )(emb, hot, rel, ids)
    far_half = call(relay_kernel, struct(far_half.shape, BF), n_in=3, anywhere=(1, 2))(
        far_half, table, other
    )
    far_rest = swapped(far_half, 1)
    theirs = call(second_kernel, columns, n_in=3)(table, rel_parts, other)
    hot_half = struct((width, hot_rows // 2), BF)
    row_half = struct((width, rows // 2), BF)
    both = (width, hot_rows // 2 + rows // 2)
    lefts, keep, send = call(
        functools.partial(edges_kernel, n_negs),
        (struct((blocks, width, per), BF), struct(both, F32), struct(both, BF)),
        scratch=[pltpu.VMEM((width, rows), BF)]
        + [pltpu.VMEM((width, hot_rows), F32), pltpu.VMEM((width, rows), F32)] * 2,
        n_in=10,
    )(far_half, far_rest, ids, *mine, other, *theirs)
    hot_sum, far_sum = call(pair_kernel, (hot_half, row_half), n_in=2)(keep, swapped(send, 1))
    arrived = home(far_sum)
    own_keep, own_send = call(
        own_kernel,
        (struct(row_half.shape, F32), row_half),
        scratch=[pltpu.VMEM((width, rows), F32)] * 2,
        n_in=4,
        anywhere=(3,),
    )(ids, other, lefts, hot_sum)
    own_got = swapped(own_send, 1)
    size = lax.axis_size("dom")
    for digit in range(size.bit_length() - 1):
        if digit > 0:
            hot_sum = call(add_kernel, hot_half, n_in=2)(hot_sum, hot_got)
        route = [(i, i ^ (1 << digit)) for i in range(size)]
        hot_got = lax.ppermute(hot_sum, "dom", route)
    own = call(own_sum_kernel, struct(row_half.shape, F32), n_in=3)(own_keep, own_got, arrived)
    return call(whole_kernel, struct((width, rows // 2 + hot_rows // 2), F32), n_in=3)(
        own, hot_sum, hot_got
    )


def four_workers(offset, arrays):
    def branch(shift):
        return functools.partial(
            bucket,
            lambda block: shifted(block, "dom", -shift),
            lambda block: shifted(block, "dom", shift),
        )

    return lax.switch(offset - 1, [branch(1), branch(2), branch(3)], *arrays)


def digit_set(offset, digit):
    return offset // (1 << digit) % 2 == 1


def many_workers(offset, arrays):
    size = lax.axis_size("dom")
    digits = size.bit_length() - 1

    def moved(block, sign):
        for digit in range(digits):
            block = jnp.where(
                digit_set(offset, digit), shifted(block, "dom", sign * (1 << digit)), block
            )
        return block

    return bucket(
        lambda block: moved(block, -1), lambda block: moved(block, 1), *arrays
    )


def body(
    plan, edge_lhs, edge_rhs, edge_rel, edge_count, negatives, emb, acc, hot_emb, hot_acc, relations
):
    emb, acc, hot, hot_acc, rel = emb.T, acc[None, :], hot_emb.T, hot_acc[None, :], relations.T
    workers = lax.axis_size("dom")
    offset = (plan[0] - lax.axis_index("dom")) % workers
    run = four_workers if workers == 4 else many_workers
    mine = run(offset, (edge_count, edge_lhs, edge_rhs, edge_rel, negatives, emb, hot, rel))
    theirs = swapped(mine, 1)
    half, half_acc = struct(mine.shape, F32), struct((1, mine.shape[1]), F32)
    ready = call(near_update_kernel, (half, half_acc, half, half_acc), n_in=5)(
        mine, emb, acc, hot, hot_acc
    )
    new_emb, new_acc, new_hot, new_hot_acc = call(
        far_update_kernel, tuple(struct(x.shape, F32) for x in (emb, acc, hot, hot_acc)), n_in=5
    )(theirs, *ready)
    return (new_emb.T, new_acc[0], new_hot.T, new_hot_acc[0])


def solution(mesh):
    placed = (
        P("dom"),
        P(("groups", "dom"), "rep"),
        P(("groups", "dom"), "rep"),
        P(("groups", "dom"), "rep"),
        P(("groups", "dom", "rep")),
        P(("groups", "dom"), "rep", None),
        P(("groups", "dom"), None),
        P(("groups", "dom")),
        P("groups", None),
        P("groups"),
        P("groups", None),
    )
    return jax.shard_map(
        body,
        mesh=mesh,
        in_specs=placed,
        out_specs=(
            P(("groups", "dom"), None),
            P(("groups", "dom")),
            P("groups", None),
            P("groups"),
        ),
        check_vma=False,
    )
```

```python
import functools

import jax
import jax.numpy as jnp
from jax import lax
from jax.experimental import pallas as pl
from jax.experimental.pallas import tpu as pltpu
from jax.sharding import PartitionSpec as P

LEARN_RATE = 0.5
BF = jnp.bfloat16
F32 = jnp.float32
LHS, RHS, REL, NEG, LIVE = 0, 1, 2, 3, 5
VMEM_LIMIT = 24 * 1024 * 1024


def call(kernel, out_shape, n_in, scratch=(), anywhere=(), smem=()):
    spaces = [
        pltpu.SMEM if i in smem else pl.ANY if i in anywhere else pltpu.VMEM for i in range(n_in)
    ]
    return pl.pallas_call(
        kernel,
        out_shape=out_shape,
        in_specs=[pl.BlockSpec(memory_space=space) for space in spaces],
        scratch_shapes=list(scratch),
        compiler_params=pltpu.CompilerParams(vmem_limit_bytes=VMEM_LIMIT),
        cost_estimate=pl.CostEstimate(flops=1, bytes_accessed=1, transcendentals=0),
    )


def dot_nt(a, b):
    return lax.dot_general(a, b, (((1,), (1,)), ((), ())), preferred_element_type=F32)


def dot_nn(a, b):
    return jnp.dot(a, b, preferred_element_type=F32)


def one_hot(ids, count):
    rows = lax.broadcasted_iota(jnp.int32, (count, ids.shape[1]), 0).astype(jnp.int16)
    return jnp.where(rows == ids.astype(jnp.int16), jnp.ones((), BF), jnp.zeros((), BF))


def fetch_all(pairs, sems):
    copies = [
        pltpu.make_async_copy(src, dst, sems.at[i]) for i, (src, dst) in enumerate(pairs)
    ]
    for copy in copies:
        copy.start()
    return copies


def halves(axis_size):
    core = lax.axis_index("rep") % 2
    cut = axis_size // 2
    return [pl.ds(pl.multiple_of(c * cut, cut), cut) for c in (core, 1 - core)]


def pack_kernel(count, emb, lhs, rhs, rel, neg, half, ids):
    half[...] = emb[:, halves(emb.shape[1])[0]].astype(BF)
    width = ids.shape[1]
    ids[...] = jnp.full(ids.shape, -1, jnp.int32)
    ids[LHS : LHS + 1, :] = lhs[...]
    ids[RHS : RHS + 1, :] = rhs[...]
    ids[REL : REL + 1, :] = rel[...]
    ids[NEG : NEG + 2, 0 : neg.shape[2]] = neg[0]
    ids[LIVE : LIVE + 1, :] = jnp.full((1, width), count[0], jnp.int32)


def count_rows(ids, counts):
    spans, rows, _ = counts.shape
    for b in range(spans):
        named = ids[NEG + b : NEG + b + 1, :]
        row_ids = lax.broadcasted_iota(jnp.int32, (rows, 128), 0)
        times = jnp.zeros((rows, 128), F32)
        for start in range(0, named.shape[1], 128):
            times += jnp.where(row_ids == named[:, start : start + 128], 1.0, 0.0)
        counts[b] = jnp.broadcast_to(jnp.sum(times, axis=1, keepdims=True), times.shape)


def list_columns(ids, table, rel_parts, query, rel_cols):
    spans, width, per = query.shape
    half = width // 2
    n_rel = rel_parts.shape[1] // 2
    rel_hot = one_hot(ids[REL : REL + 1, :], n_rel)
    rel_all = dot_nn(rel_parts[:, :n_rel], rel_hot) + dot_nn(rel_parts[:, n_rel:], rel_hot)
    left_all = dot_nn(table[...], one_hot(ids[LHS : LHS + 1, :], table.shape[1]))
    for b in range(spans):
        lanes = slice(b * per, (b + 1) * per)
        left, rel_col = left_all[:, lanes], rel_all[:, lanes]
        rel_cols[b] = rel_col
        l_re, l_im = left[:half], left[half:]
        r_re, r_im = rel_col[:half], rel_col[half:]
        query[b, :half] = (l_re * r_re - l_im * r_im).astype(BF)
        query[b, half:] = (l_re * r_im + l_im * r_re).astype(BF)


def first_kernel(
    emb, hot, rel, ids, table, rel_parts, query, rel_cols, counts, emb_s, hot_s, rel_s, sems
):
    copies = fetch_all([(emb, emb_s), (hot, hot_s), (rel, rel_s)], sems)
    count_rows(ids, counts)
    rows = emb.shape[1]
    copies[0].wait()
    table[:, :rows] = emb_s[...].astype(BF)
    copies[1].wait()
    table[:, rows:] = hot_s[...].astype(BF)
    copies[2].wait()
    n_rel = rel.shape[1]
    high = rel_s[...].astype(BF)
    rel_parts[:, :n_rel] = high
    rel_parts[:, n_rel:] = (rel_s[...] - high.astype(F32)).astype(BF)
    list_columns(ids, table, rel_parts, query, rel_cols)


def second_kernel(table, rel_parts, ids, query, rel_cols, counts):
    count_rows(ids, counts)
    list_columns(ids, table, rel_parts, query, rel_cols)


def relay_kernel(one, after, other, out):
    del after, other
    out[...] = one[...]


def edges_kernel(n_negs, far_half, far_rest, *refs):
    lists = (refs[0:4], refs[4:8])
    lefts, keep, send, far, *totals = refs[8:]
    mine, theirs = halves(far.shape[1])
    far[:, mine] = far_half[...]
    far[:, theirs] = far_rest[...]
    rows = far.shape[1]
    hot_rows = totals[0].shape[1]
    far_t = far[...].astype(F32).T.astype(BF)
    work = []
    for i, (ids, query, rel_cols, counts) in enumerate(lists):
        for b in range(query.shape[0]):
            work.append((i, b, dot_nn(far_t, query[b])))
    spans, width, per = lists[0][1].shape
    half = width // 2
    row_ids = lax.broadcasted_iota(jnp.int32, (rows, per), 0)
    done = []
    for i, b, scores in work:
        ids, query, rel_cols, counts = lists[i]
        lanes = slice(b * per, (b + 1) * per)
        right = row_ids == ids[RHS : RHS + 1, lanes]
        place = lax.broadcasted_iota(jnp.int32, (1, per), 1) + b * per
        mask = jnp.where(place < ids[LIVE : LIVE + 1, lanes], 1.0, 0.0)
        chance = 0.5 * jnp.tanh(0.5 * scores) + 0.5
        times = jnp.concatenate([counts[b]] * (per // 128), axis=1)
        grad = (chance * (mask / n_negs)).astype(BF).astype(F32) * times
        grad = (grad + jnp.where(right, (chance - 1.0) * mask, 0.0)).astype(BF)
        done.append((i, b, grad))
    for i, b, grad in done:
        ids, query, rel_cols, counts = lists[i]
        at = i * spans + b
        lanes = slice(b * per, (b + 1) * per)
        gq = dot_nn(far[...], grad)
        r_re, r_im = rel_cols[b, :half], rel_cols[b, half:]
        g_re, g_im = gq[:half], gq[half:]
        lefts[at, :half] = (g_re * r_re + g_im * r_im).astype(BF)
        lefts[at, half:] = (g_im * r_re - g_re * r_im).astype(BF)
        add_far = dot_nt(query[b], grad)
        hot_total, far_total = totals[2 * i : 2 * i + 2]
        if b == 0:
            far_total[...] = add_far
        else:
            far_total[...] += add_far
    for i, b, grad in done:
        ids, query, rel_cols, counts = lists[i]
        at = i * spans + b
        lanes = slice(b * per, (b + 1) * per)
        hot_total, far_total = totals[2 * i : 2 * i + 2]
        left_hot = one_hot(ids[LHS : LHS + 1, lanes] - rows, hot_rows)
        add_hot = dot_nt(lefts[at], left_hot)
        if b == 0:
            hot_total[...] = add_hot
        else:
            hot_total[...] += add_hot
    cut = hot_rows // 2
    for j, (mine, theirs) in enumerate((halves(hot_rows), halves(rows))):
        lanes = slice(0, cut) if j == 0 else slice(cut, cut + rows // 2)
        keep[:, lanes] = totals[j][:, mine] + totals[2 + j][:, mine]
        send[:, lanes] = (totals[j][:, theirs] + totals[2 + j][:, theirs]).astype(BF)


def own_kernel(ids_0, ids_1, lefts, after, keep, send, *totals):
    del after
    per = lefts.shape[2]
    rows = totals[0].shape[1]
    for i, ids in enumerate((ids_0, ids_1)):
        spans = lefts.shape[0] // 2
        for b in range(spans):
            left_own = one_hot(ids[LHS : LHS + 1, b * per : (b + 1) * per], rows)
            add = dot_nt(lefts[i * spans + b], left_own)
            if b == 0:
                totals[i][...] = add
            else:
                totals[i][...] += add
    mine, theirs = halves(rows)
    keep[...] = totals[0][:, mine] + totals[1][:, mine]
    send[...] = (totals[0][:, theirs] + totals[1][:, theirs]).astype(BF)


def pair_kernel(keep, got, hot, far):
    total = (keep[...] + got[...].astype(F32)).astype(BF)
    cut = hot.shape[1]
    hot[...] = total[:, :cut]
    far[...] = total[:, cut:]


def add_kernel(one, other, out):
    out[...] = (one[...].astype(F32) + other[...].astype(F32)).astype(BF)


def own_sum_kernel(keep, got, far, out):
    out[...] = (keep[...] + got[...].astype(F32)) + far[...].astype(F32)


def whole_kernel(own, one, other, out):
    cut = own.shape[1]
    out[:, :cut] = own[...]
    out[:, cut:] = one[...].astype(F32) + other[...].astype(F32)


def adagrad(weights, accum, grad):
    new = accum + jnp.sum(grad * grad, axis=0, keepdims=True) / grad.shape[0]
    return weights - LEARN_RATE * grad / jnp.sqrt(new), new


def near_update_kernel(grads, emb, acc, hot, hot_acc, done, done_acc, rest, rest_acc):
    cut = grads.shape[1] // 2
    mine, theirs = halves(2 * cut)
    for i, (w, a) in enumerate(((emb, acc), (hot, hot_acc))):
        lanes = slice(i * cut, (i + 1) * cut)
        done[:, lanes], done_acc[:, lanes] = adagrad(w[:, mine], a[:, mine], grads[:, lanes])
        rest[:, lanes] = w[:, theirs]
        rest_acc[:, lanes] = a[:, theirs]


def far_update_kernel(grads, done, done_acc, rest, rest_acc, emb, acc, hot, hot_acc):
    cut = grads.shape[1] // 2
    mine, theirs = halves(2 * cut)
    for i, (w, a) in enumerate(((emb, acc), (hot, hot_acc))):
        lanes = slice(i * cut, (i + 1) * cut)
        w[:, mine] = done[:, lanes]
        a[:, mine] = done_acc[:, lanes]
        w[:, theirs], a[:, theirs] = adagrad(rest[:, lanes], rest_acc[:, lanes], grads[:, lanes])


def shifted(block, axis, distance):
    size = lax.axis_size(axis)
    return lax.ppermute(block, axis, [((i - distance) % size, i) for i in range(size)])


def swapped(block, bit):
    return lax.ppermute(block, "rep", [(i, i ^ bit) for i in range(lax.axis_size("rep"))])


def struct(shape, dtype):
    return jax.ShapeDtypeStruct(shape, dtype)


def bucket(fetch, home, count, lhs, rhs, rel_ids, neg, emb, hot, rel):
    width, rows = emb.shape
    hot_rows = hot.shape[1]
    edges = lhs.shape[1]
    spans, n_negs = neg.shape[1:]
    per = edges // spans
    blocks = 2 * spans
    emb_half, ids = call(
        pack_kernel,
        (struct((width, rows // 2), BF), struct((8, edges), jnp.int32)),
        n_in=6,
        smem=(0,),
    )(count, emb, lhs, rhs, rel_ids, neg)
    far_half = fetch(emb_half)
    other = swapped(ids, 2)
    columns = (
        struct((spans, width, per), BF),
        struct((spans, width, per), F32),
        struct((spans, rows, 128), F32),
    )
    table, rel_parts, *mine = call(
        first_kernel,
        (struct((width, rows + hot_rows), BF), struct((width, 2 * rel.shape[1]), BF), *columns),
        n_in=4,
        anywhere=(0, 1, 2),
        scratch=[pltpu.VMEM(x.shape, F32) for x in (emb, hot, rel)] + [pltpu.SemaphoreType.DMA((3,))],
    )(emb, hot, rel, ids)
    far_half = call(relay_kernel, struct(far_half.shape, BF), n_in=3, anywhere=(1, 2))(
        far_half, table, other
    )
    far_rest = swapped(far_half, 1)
    theirs = call(second_kernel, columns, n_in=3)(table, rel_parts, other)
    hot_half = struct((width, hot_rows // 2), BF)
    row_half = struct((width, rows // 2), BF)
    both = (width, hot_rows // 2 + rows // 2)
    lefts, keep, send = call(
        functools.partial(edges_kernel, n_negs),
        (struct((blocks, width, per), BF), struct(both, F32), struct(both, BF)),
        scratch=[pltpu.VMEM((width, rows), BF)]
        + [pltpu.VMEM((width, hot_rows), F32), pltpu.VMEM((width, rows), F32)] * 2,
        n_in=10,
    )(far_half, far_rest, ids, *mine, other, *theirs)
    hot_sum, far_sum = call(pair_kernel, (hot_half, row_half), n_in=2)(keep, swapped(send, 1))
    arrived = home(far_sum)
    own_keep, own_send = call(
        own_kernel,
        (struct(row_half.shape, F32), row_half),
        scratch=[pltpu.VMEM((width, rows), F32)] * 2,
        n_in=4,
        anywhere=(3,),
    )(ids, other, lefts, hot_sum)
    own_got = swapped(own_send, 1)
    size = lax.axis_size("dom")
    for digit in range(size.bit_length() - 1):
        if digit > 0:
            hot_sum = call(add_kernel, hot_half, n_in=2)(hot_sum, hot_got)
        route = [(i, i ^ (1 << digit)) for i in range(size)]
        hot_got = lax.ppermute(hot_sum, "dom", route)
    own = call(own_sum_kernel, struct(row_half.shape, F32), n_in=3)(own_keep, own_got, arrived)
    return call(whole_kernel, struct((width, rows // 2 + hot_rows // 2), F32), n_in=3)(
        own, hot_sum, hot_got
    )


def four_workers(offset, arrays):
    def branch(shift):
        return functools.partial(
            bucket,
            lambda block: shifted(block, "dom", -shift),
            lambda block: shifted(block, "dom", shift),
        )

    return lax.switch(offset - 1, [branch(1), branch(2), branch(3)], *arrays)


def digit_set(offset, digit):
    return offset // (1 << digit) % 2 == 1


def many_workers(offset, arrays):
    size = lax.axis_size("dom")
    digits = size.bit_length() - 1

    def moved(block, sign):
        for digit in range(digits):
            block = jnp.where(
                digit_set(offset, digit), shifted(block, "dom", sign * (1 << digit)), block
            )
        return block

    return bucket(
        lambda block: moved(block, -1), lambda block: moved(block, 1), *arrays
    )


def body(
    plan, edge_lhs, edge_rhs, edge_rel, edge_count, negatives, emb, acc, hot_emb, hot_acc, relations
):
    emb, acc, hot, hot_acc, rel = emb.T, acc[None, :], hot_emb.T, hot_acc[None, :], relations.T
    workers = lax.axis_size("dom")
    offset = (plan[0] - lax.axis_index("dom")) % workers
    run = four_workers if workers == 4 else many_workers
    mine = run(offset, (edge_count, edge_lhs, edge_rhs, edge_rel, negatives, emb, hot, rel))
    theirs = swapped(mine, 1)
    half, half_acc = struct(mine.shape, F32), struct((1, mine.shape[1]), F32)
    ready = call(near_update_kernel, (half, half_acc, half, half_acc), n_in=5)(
        mine, emb, acc, hot, hot_acc
    )
    new_emb, new_acc, new_hot, new_hot_acc = call(
        far_update_kernel, tuple(struct(x.shape, F32) for x in (emb, acc, hot, hot_acc)), n_in=5
    )(theirs, *ready)
    return (new_emb.T, new_acc[0], new_hot.T, new_hot_acc[0])


def solution(mesh):
    placed = (
        P("dom"),
        P(("groups", "dom"), "rep"),
        P(("groups", "dom"), "rep"),
        P(("groups", "dom"), "rep"),
        P(("groups", "dom", "rep")),
        P(("groups", "dom"), "rep", None),
        P(("groups", "dom"), None),
        P(("groups", "dom")),
        P("groups", None),
        P("groups"),
        P("groups", None),
    )
    return jax.shard_map(
        body,
        mesh=mesh,
        in_specs=placed,
        out_specs=(
            P(("groups", "dom"), None),
            P(("groups", "dom")),
            P("groups", None),
            P("groups"),
        ),
        check_vma=False,
    )
```

```python
import functools

import jax
import jax.numpy as jnp
from jax import lax
from jax.experimental import pallas as pl
from jax.experimental.pallas import tpu as pltpu
from jax.sharding import PartitionSpec as P

LEARN_RATE = 0.5
BF = jnp.bfloat16
F32 = jnp.float32
LHS, RHS, REL, NEG, LIVE = 0, 1, 2, 3, 5
VMEM_LIMIT = 24 * 1024 * 1024


def call(kernel, out_shape, n_in, scratch=(), anywhere=(), smem=()):
    spaces = [
        pltpu.SMEM if i in smem else pl.ANY if i in anywhere else pltpu.VMEM for i in range(n_in)
    ]
    return pl.pallas_call(
        kernel,
        out_shape=out_shape,
        in_specs=[pl.BlockSpec(memory_space=space) for space in spaces],
        scratch_shapes=list(scratch),
        compiler_params=pltpu.CompilerParams(vmem_limit_bytes=VMEM_LIMIT),
        cost_estimate=pl.CostEstimate(flops=1, bytes_accessed=1, transcendentals=0),
    )


def dot_nt(a, b):
    return lax.dot_general(a, b, (((1,), (1,)), ((), ())), preferred_element_type=F32)


def dot_nn(a, b):
    return jnp.dot(a, b, preferred_element_type=F32)


def one_hot(ids, count):
    rows = lax.broadcasted_iota(jnp.int32, (count, ids.shape[1]), 0).astype(jnp.int16)
    return jnp.where(rows == ids.astype(jnp.int16), jnp.ones((), BF), jnp.zeros((), BF))


def fetch_all(pairs, sems):
    copies = [
        pltpu.make_async_copy(src, dst, sems.at[i]) for i, (src, dst) in enumerate(pairs)
    ]
    for copy in copies:
        copy.start()
    return copies


def halves(axis_size):
    core = lax.axis_index("rep") % 2
    cut = axis_size // 2
    return [pl.ds(pl.multiple_of(c * cut, cut), cut) for c in (core, 1 - core)]


def pack_kernel(count, emb, lhs, rhs, rel, neg, half, ids):
    half[...] = emb[:, halves(emb.shape[1])[0]].astype(BF)
    width = ids.shape[1]
    ids[...] = jnp.full(ids.shape, -1, jnp.int32)
    ids[LHS : LHS + 1, :] = lhs[...]
    ids[RHS : RHS + 1, :] = rhs[...]
    ids[REL : REL + 1, :] = rel[...]
    ids[NEG : NEG + 2, 0 : neg.shape[2]] = neg[0]
    ids[LIVE : LIVE + 1, :] = jnp.full((1, width), count[0], jnp.int32)


def count_rows(ids, counts):
    spans, rows, _ = counts.shape
    for b in range(spans):
        named = ids[NEG + b : NEG + b + 1, :]
        row_ids = lax.broadcasted_iota(jnp.int32, (rows, 128), 0)
        times = jnp.zeros((rows, 128), F32)
        for start in range(0, named.shape[1], 128):
            times += jnp.where(row_ids == named[:, start : start + 128], 1.0, 0.0)
        counts[b] = jnp.broadcast_to(jnp.sum(times, axis=1, keepdims=True), times.shape)


def list_columns(ids, table, rel_parts, query, rel_cols):
    spans, width, per = query.shape
    half = width // 2
    n_rel = rel_parts.shape[1] // 2
    rel_hot = one_hot(ids[REL : REL + 1, :], n_rel)
    rel_all = dot_nn(rel_parts[:, :n_rel], rel_hot) + dot_nn(rel_parts[:, n_rel:], rel_hot)
    left_all = dot_nn(table[...], one_hot(ids[LHS : LHS + 1, :], table.shape[1]))
    for b in range(spans):
        lanes = slice(b * per, (b + 1) * per)
        left, rel_col = left_all[:, lanes], rel_all[:, lanes]
        rel_cols[b] = rel_col
        l_re, l_im = left[:half], left[half:]
        r_re, r_im = rel_col[:half], rel_col[half:]
        query[b, :half] = (l_re * r_re - l_im * r_im).astype(BF)
        query[b, half:] = (l_re * r_im + l_im * r_re).astype(BF)


def first_kernel(
    emb, hot, rel, ids, table, rel_parts, query, rel_cols, counts, emb_s, hot_s, rel_s, sems
):
    copies = fetch_all([(emb, emb_s), (hot, hot_s), (rel, rel_s)], sems)
    count_rows(ids, counts)
    rows = emb.shape[1]
    copies[0].wait()
    table[:, :rows] = emb_s[...].astype(BF)
    copies[1].wait()
    table[:, rows:] = hot_s[...].astype(BF)
    copies[2].wait()
    n_rel = rel.shape[1]
    high = rel_s[...].astype(BF)
    rel_parts[:, :n_rel] = high
    rel_parts[:, n_rel:] = (rel_s[...] - high.astype(F32)).astype(BF)
    list_columns(ids, table, rel_parts, query, rel_cols)


def second_kernel(table, rel_parts, ids, query, rel_cols, counts):
    count_rows(ids, counts)
    list_columns(ids, table, rel_parts, query, rel_cols)


def relay_kernel(one, after, other, out):
    del after, other
    out[...] = one[...]


def edges_kernel(n_negs, far_half, far_rest, *refs):
    lists = (refs[0:4], refs[4:8])
    lefts, keep, send, far, *totals = refs[8:]
    mine, theirs = halves(far.shape[1])
    far[:, mine] = far_half[...]
    far[:, theirs] = far_rest[...]
    rows = far.shape[1]
    hot_rows = totals[0].shape[1]
    far_t = far[...].astype(F32).T.astype(BF)
    work = []
    for i, (ids, query, rel_cols, counts) in enumerate(lists):
        for b in range(query.shape[0]):
            work.append((i, b, dot_nn(far_t, query[b])))
    spans, width, per = lists[0][1].shape
    half = width // 2
    row_ids = lax.broadcasted_iota(jnp.int32, (rows, per), 0)
    done = []
    for i, b, scores in work:
        ids, query, rel_cols, counts = lists[i]
        lanes = slice(b * per, (b + 1) * per)
        right = row_ids == ids[RHS : RHS + 1, lanes]
        place = lax.broadcasted_iota(jnp.int32, (1, per), 1) + b * per
        mask = jnp.where(place < ids[LIVE : LIVE + 1, lanes], 1.0, 0.0)
        chance = 0.5 * jnp.tanh(0.5 * scores) + 0.5
        times = jnp.concatenate([counts[b]] * (per // 128), axis=1)
        grad = (chance * (mask / n_negs)).astype(BF).astype(F32) * times
        grad = (grad + jnp.where(right, (chance - 1.0) * mask, 0.0)).astype(BF)
        done.append((i, b, grad))
    for i, b, grad in done:
        ids, query, rel_cols, counts = lists[i]
        at = i * spans + b
        lanes = slice(b * per, (b + 1) * per)
        gq = dot_nn(far[...], grad)
        r_re, r_im = rel_cols[b, :half], rel_cols[b, half:]
        g_re, g_im = gq[:half], gq[half:]
        lefts[at, :half] = (g_re * r_re + g_im * r_im).astype(BF)
        lefts[at, half:] = (g_im * r_re - g_re * r_im).astype(BF)
        add_far = dot_nt(query[b], grad)
        hot_total, far_total = totals[2 * i : 2 * i + 2]
        if b == 0:
            far_total[...] = add_far
        else:
            far_total[...] += add_far
    for i, b, grad in done:
        ids, query, rel_cols, counts = lists[i]
        at = i * spans + b
        lanes = slice(b * per, (b + 1) * per)
        hot_total, far_total = totals[2 * i : 2 * i + 2]
        left_hot = one_hot(ids[LHS : LHS + 1, lanes] - rows, hot_rows)
        add_hot = dot_nt(lefts[at], left_hot)
        if b == 0:
            hot_total[...] = add_hot
        else:
            hot_total[...] += add_hot
    cut = hot_rows // 2
    for j, (mine, theirs) in enumerate((halves(hot_rows), halves(rows))):
        lanes = slice(0, cut) if j == 0 else slice(cut, cut + rows // 2)
        keep[:, lanes] = totals[j][:, mine] + totals[2 + j][:, mine]
        send[:, lanes] = (totals[j][:, theirs] + totals[2 + j][:, theirs]).astype(BF)


def own_kernel(ids_0, ids_1, lefts, far_in, keep, send, far, *totals):
    far[...] = far_in[...]
    per = lefts.shape[2]
    rows = totals[0].shape[1]
    for i, ids in enumerate((ids_0, ids_1)):
        spans = lefts.shape[0] // 2
        for b in range(spans):
            left_own = one_hot(ids[LHS : LHS + 1, b * per : (b + 1) * per], rows)
            add = dot_nt(lefts[i * spans + b], left_own)
            if b == 0:
                totals[i][...] = add
            else:
                totals[i][...] += add
    mine, theirs = halves(rows)
    keep[...] = totals[0][:, mine] + totals[1][:, mine]
    send[...] = (totals[0][:, theirs] + totals[1][:, theirs]).astype(BF)


def pair_kernel(keep, got, hot, far):
    cut = hot.shape[1]
    hot[...] = (keep[:, :cut] + got[:, :cut].astype(F32)).astype(BF)
    part = far.shape[0]
    at = pl.ds(pl.multiple_of(lax.axis_index("rep") // 2 * (hot.shape[0] - part), 16), part)
    far[...] = (keep[at, cut:] + got[at, cut:].astype(F32)).astype(BF)


def add_kernel(one, other, out):
    out[...] = (one[...].astype(F32) + other[...].astype(F32)).astype(BF)


def own_sum_kernel(keep, got, far, far_other, out):
    first = lax.axis_index("rep") // 2 == 0
    low = jnp.where(first, far[...].astype(F32), far_other[...].astype(F32))
    high = jnp.where(first, far_other[...].astype(F32), far[...].astype(F32))
    part = low.shape[0]
    over = 2 * part - out.shape[0]
    total = keep[...] + got[...].astype(F32)
    out[:part] = total[:part] + low
    out[part:] = total[part:] + high[over:]


def whole_kernel(own, one, other, out):
    cut = own.shape[1]
    out[:, :cut] = own[...]
    out[:, cut:] = one[...].astype(F32) + other[...].astype(F32)


def adagrad(weights, accum, grad):
    new = accum + jnp.sum(grad * grad, axis=0, keepdims=True) / grad.shape[0]
    return weights - LEARN_RATE * grad / jnp.sqrt(new), new


def near_update_kernel(grads, emb, acc, hot, hot_acc, done, done_acc, rest, rest_acc):
    cut = grads.shape[1] // 2
    mine, theirs = halves(2 * cut)
    for i, (w, a) in enumerate(((emb, acc), (hot, hot_acc))):
        lanes = slice(i * cut, (i + 1) * cut)
        done[:, lanes], done_acc[:, lanes] = adagrad(w[:, mine], a[:, mine], grads[:, lanes])
        rest[:, lanes] = w[:, theirs]
        rest_acc[:, lanes] = a[:, theirs]


def far_update_kernel(grads, done, done_acc, rest, rest_acc, emb, acc, hot, hot_acc):
    cut = grads.shape[1] // 2
    mine, theirs = halves(2 * cut)
    for i, (w, a) in enumerate(((emb, acc), (hot, hot_acc))):
        lanes = slice(i * cut, (i + 1) * cut)
        w[:, mine] = done[:, lanes]
        a[:, mine] = done_acc[:, lanes]
        w[:, theirs], a[:, theirs] = adagrad(rest[:, lanes], rest_acc[:, lanes], grads[:, lanes])


def shifted(block, axis, distance):
    size = lax.axis_size(axis)
    return lax.ppermute(block, axis, [((i - distance) % size, i) for i in range(size)])


def swapped(block, bit):
    return lax.ppermute(block, "rep", [(i, i ^ bit) for i in range(lax.axis_size("rep"))])


def struct(shape, dtype):
    return jax.ShapeDtypeStruct(shape, dtype)


def bucket(fetch, home, count, lhs, rhs, rel_ids, neg, emb, hot, rel):
    width, rows = emb.shape
    hot_rows = hot.shape[1]
    edges = lhs.shape[1]
    spans, n_negs = neg.shape[1:]
    per = edges // spans
    blocks = 2 * spans
    emb_half, ids = call(
        pack_kernel,
        (struct((width, rows // 2), BF), struct((8, edges), jnp.int32)),
        n_in=6,
        smem=(0,),
    )(count, emb, lhs, rhs, rel_ids, neg)
    far_half = fetch(emb_half)
    other = swapped(ids, 2)
    columns = (
        struct((spans, width, per), BF),
        struct((spans, width, per), F32),
        struct((spans, rows, 128), F32),
    )
    table, rel_parts, *mine = call(
        first_kernel,
        (struct((width, rows + hot_rows), BF), struct((width, 2 * rel.shape[1]), BF), *columns),
        n_in=4,
        anywhere=(0, 1, 2),
        scratch=[pltpu.VMEM(x.shape, F32) for x in (emb, hot, rel)] + [pltpu.SemaphoreType.DMA((3,))],
    )(emb, hot, rel, ids)
    far_half = call(relay_kernel, struct(far_half.shape, BF), n_in=3, anywhere=(1, 2))(
        far_half, table, other
    )
    far_rest = swapped(far_half, 1)
    theirs = call(second_kernel, columns, n_in=3)(table, rel_parts, other)
    hot_half = struct((width, hot_rows // 2), BF)
    row_half = struct((width, rows // 2), BF)
    both = (width, hot_rows // 2 + rows // 2)
    lefts, keep, send = call(
        functools.partial(edges_kernel, n_negs),
        (struct((blocks, width, per), BF), struct(both, F32), struct(both, BF)),
        scratch=[pltpu.VMEM((width, rows), BF)]
        + [pltpu.VMEM((width, hot_rows), F32), pltpu.VMEM((width, rows), F32)] * 2,
        n_in=10,
    )(far_half, far_rest, ids, *mine, other, *theirs)
    part = struct((-(-width // 32) * 16, rows // 2), BF)
    hot_sum, far_sum = call(pair_kernel, (hot_half, part), n_in=2)(keep, swapped(send, 1))
    own_keep, own_send, far_sum = call(
        own_kernel,
        (struct(row_half.shape, F32), row_half, part),
        scratch=[pltpu.VMEM((width, rows), F32)] * 2,
        n_in=4,
    )(ids, other, lefts, far_sum)
    arrived = home(far_sum)
    arrived_other = swapped(arrived, 2)
    own_got = swapped(own_send, 1)
    size = lax.axis_size("dom")
    for digit in range(size.bit_length() - 1):
        if digit > 0:
            hot_sum = call(add_kernel, hot_half, n_in=2)(hot_sum, hot_got)
        route = [(i, i ^ (1 << digit)) for i in range(size)]
        hot_got = lax.ppermute(hot_sum, "dom", route)
    own = call(own_sum_kernel, struct(row_half.shape, F32), n_in=4)(
        own_keep, own_got, arrived, arrived_other
    )
    return call(whole_kernel, struct((width, rows // 2 + hot_rows // 2), F32), n_in=3)(
        own, hot_sum, hot_got
    )


def four_workers(offset, arrays):
    def branch(shift):
        return functools.partial(
            bucket,
            lambda block: shifted(block, "dom", -shift),
            lambda block: shifted(block, "dom", shift),
        )

    return lax.switch(offset - 1, [branch(1), branch(2), branch(3)], *arrays)


def digit_set(offset, digit):
    return offset // (1 << digit) % 2 == 1


def many_workers(offset, arrays):
    size = lax.axis_size("dom")
    digits = size.bit_length() - 1

    def moved(block, sign):
        for digit in range(digits):
            block = jnp.where(
                digit_set(offset, digit), shifted(block, "dom", sign * (1 << digit)), block
            )
        return block

    return bucket(
        lambda block: moved(block, -1), lambda block: moved(block, 1), *arrays
    )


def body(
    plan, edge_lhs, edge_rhs, edge_rel, edge_count, negatives, emb, acc, hot_emb, hot_acc, relations
):
    emb, acc, hot, hot_acc, rel = emb.T, acc[None, :], hot_emb.T, hot_acc[None, :], relations.T
    workers = lax.axis_size("dom")
    offset = (plan[0] - lax.axis_index("dom")) % workers
    run = four_workers if workers == 4 else many_workers
    mine = run(offset, (edge_count, edge_lhs, edge_rhs, edge_rel, negatives, emb, hot, rel))
    theirs = swapped(mine, 1)
    half, half_acc = struct(mine.shape, F32), struct((1, mine.shape[1]), F32)
    ready = call(near_update_kernel, (half, half_acc, half, half_acc), n_in=5)(
        mine, emb, acc, hot, hot_acc
    )
    new_emb, new_acc, new_hot, new_hot_acc = call(
        far_update_kernel, tuple(struct(x.shape, F32) for x in (emb, acc, hot, hot_acc)), n_in=5
    )(theirs, *ready)
    return (new_emb.T, new_acc[0], new_hot.T, new_hot_acc[0])


def solution(mesh):
    placed = (
        P("dom"),
        P(("groups", "dom"), "rep"),
        P(("groups", "dom"), "rep"),
        P(("groups", "dom"), "rep"),
        P(("groups", "dom", "rep")),
        P(("groups", "dom"), "rep", None),
        P(("groups", "dom"), None),
        P(("groups", "dom")),
        P("groups", None),
        P("groups"),
        P("groups", None),
    )
    return jax.shard_map(
        body,
        mesh=mesh,
        in_specs=placed,
        out_specs=(
            P(("groups", "dom"), None),
            P(("groups", "dom")),
            P("groups", None),
            P("groups"),
        ),
        check_vma=False,
    )
```

```python
import functools

import jax
import jax.numpy as jnp
from jax import lax
from jax.experimental import pallas as pl
from jax.experimental.pallas import tpu as pltpu
from jax.sharding import PartitionSpec as P

LEARN_RATE = 0.5
BF = jnp.bfloat16
F32 = jnp.float32
LHS, RHS, REL, NEG, LIVE = 0, 1, 2, 3, 5
VMEM_LIMIT = 24 * 1024 * 1024


def call(kernel, out_shape, n_in, scratch=(), anywhere=(), smem=()):
    spaces = [
        pltpu.SMEM if i in smem else pl.ANY if i in anywhere else pltpu.VMEM for i in range(n_in)
    ]
    return pl.pallas_call(
        kernel,
        out_shape=out_shape,
        in_specs=[pl.BlockSpec(memory_space=space) for space in spaces],
        scratch_shapes=list(scratch),
        compiler_params=pltpu.CompilerParams(vmem_limit_bytes=VMEM_LIMIT),
        cost_estimate=pl.CostEstimate(flops=1, bytes_accessed=1, transcendentals=0),
    )


def dot_nt(a, b):
    return lax.dot_general(a, b, (((1,), (1,)), ((), ())), preferred_element_type=F32)


def dot_nn(a, b):
    return jnp.dot(a, b, preferred_element_type=F32)


def one_hot(ids, count):
    rows = lax.broadcasted_iota(jnp.int32, (count, ids.shape[1]), 0).astype(jnp.int16)
    return jnp.where(rows == ids.astype(jnp.int16), jnp.ones((), BF), jnp.zeros((), BF))


def halves(axis_size):
    core = lax.axis_index("rep") % 2
    cut = axis_size // 2
    return [pl.ds(pl.multiple_of(c * cut, cut), cut) for c in (core, 1 - core)]


def pack_kernel(emb, lhs, rhs, rel, neg, hot, relations, half, ids):
    del hot, relations
    half[...] = emb[:, halves(emb.shape[1])[0]].astype(BF)
    ids[...] = jnp.full(ids.shape, -1, jnp.int32)
    ids[LHS : LHS + 1, :] = lhs[...]
    ids[RHS : RHS + 1, :] = rhs[...]
    ids[REL : REL + 1, :] = rel[...]
    ids[NEG : NEG + 2, 0 : neg.shape[2]] = neg[0]


def live_kernel(count, ids, out):
    out[...] = ids[...]
    out[LIVE : LIVE + 1, :] = jnp.full((1, ids.shape[1]), count[0], jnp.int32)


def count_rows(ids, counts):
    spans, rows, _ = counts.shape
    for b in range(spans):
        named = ids[NEG + b : NEG + b + 1, :]
        row_ids = lax.broadcasted_iota(jnp.int32, (rows, 128), 0)
        times = jnp.zeros((rows, 128), F32)
        for start in range(0, named.shape[1], 128):
            times += jnp.where(row_ids == named[:, start : start + 128], 1.0, 0.0)
        counts[b] = jnp.broadcast_to(jnp.sum(times, axis=1, keepdims=True), times.shape)


def list_columns(ids, table, rel_parts, query, rel_cols):
    spans, width, per = query.shape
    half = width // 2
    n_rel = rel_parts.shape[1] // 2
    rel_hot = one_hot(ids[REL : REL + 1, :], n_rel)
    rel_all = dot_nn(rel_parts[:, :n_rel], rel_hot) + dot_nn(rel_parts[:, n_rel:], rel_hot)
    left_all = dot_nn(table[...], one_hot(ids[LHS : LHS + 1, :], table.shape[1]))
    for b in range(spans):
        lanes = slice(b * per, (b + 1) * per)
        left, rel_col = left_all[:, lanes], rel_all[:, lanes]
        rel_cols[b] = rel_col
        l_re, l_im = left[:half], left[half:]
        r_re, r_im = rel_col[:half], rel_col[half:]
        query[b, :half] = (l_re * r_re - l_im * r_im).astype(BF)
        query[b, half:] = (l_re * r_im + l_im * r_re).astype(BF)


def first_kernel(emb, hot, rel, ids, table, rel_parts, query, rel_cols, counts):
    count_rows(ids, counts)
    rows = emb.shape[1]
    table[:, :rows] = emb[...].astype(BF)
    table[:, rows:] = hot[...].astype(BF)
    n_rel = rel.shape[1]
    high = rel[...].astype(BF)
    rel_parts[:, :n_rel] = high
    rel_parts[:, n_rel:] = (rel[...] - high.astype(F32)).astype(BF)
    list_columns(ids, table, rel_parts, query, rel_cols)


def second_kernel(table, rel_parts, ids, query, rel_cols, counts):
    count_rows(ids, counts)
    list_columns(ids, table, rel_parts, query, rel_cols)


def relay_kernel(one, after, other, out):
    del after, other
    out[...] = one[...]


def edges_kernel(n_negs, far_half, far_rest, *refs):
    lists = (refs[0:4], refs[4:8])
    lefts, keep, send, far, *totals = refs[8:]
    mine, theirs = halves(far.shape[1])
    far[:, mine] = far_half[...]
    far[:, theirs] = far_rest[...]
    rows = far.shape[1]
    hot_rows = totals[0].shape[1]
    far_t = far[...].astype(F32).T.astype(BF)
    work = []
    for i, (ids, query, rel_cols, counts) in enumerate(lists):
        for b in range(query.shape[0]):
            work.append((i, b, dot_nn(far_t, query[b])))
    spans, width, per = lists[0][1].shape
    half = width // 2
    row_ids = lax.broadcasted_iota(jnp.int32, (rows, per), 0)
    done = []
    for i, b, scores in work:
        ids, query, rel_cols, counts = lists[i]
        lanes = slice(b * per, (b + 1) * per)
        right = row_ids == ids[RHS : RHS + 1, lanes]
        place = lax.broadcasted_iota(jnp.int32, (1, per), 1) + b * per
        mask = jnp.where(place < ids[LIVE : LIVE + 1, lanes], 1.0, 0.0)
        chance = 0.5 * jnp.tanh(0.5 * scores) + 0.5
        times = jnp.concatenate([counts[b]] * (per // 128), axis=1)
        grad = (chance * (mask / n_negs)).astype(BF).astype(F32) * times
        grad = (grad + jnp.where(right, (chance - 1.0) * mask, 0.0)).astype(BF)
        done.append((i, b, grad))
    for i, b, grad in done:
        ids, query, rel_cols, counts = lists[i]
        at = i * spans + b
        lanes = slice(b * per, (b + 1) * per)
        gq = dot_nn(far[...], grad)
        r_re, r_im = rel_cols[b, :half], rel_cols[b, half:]
        g_re, g_im = gq[:half], gq[half:]
        lefts[at, :half] = (g_re * r_re + g_im * r_im).astype(BF)
        lefts[at, half:] = (g_im * r_re - g_re * r_im).astype(BF)
        add_far = dot_nt(query[b], grad)
        hot_total, far_total = totals[2 * i : 2 * i + 2]
        if b == 0:
            far_total[...] = add_far
        else:
            far_total[...] += add_far
    for i, b, grad in done:
        ids, query, rel_cols, counts = lists[i]
        at = i * spans + b
        lanes = slice(b * per, (b + 1) * per)
        hot_total, far_total = totals[2 * i : 2 * i + 2]
        left_hot = one_hot(ids[LHS : LHS + 1, lanes] - rows, hot_rows)
        add_hot = dot_nt(lefts[at], left_hot)
        if b == 0:
            hot_total[...] = add_hot
        else:
            hot_total[...] += add_hot
    cut = hot_rows // 2
    for j, (mine, theirs) in enumerate((halves(hot_rows), halves(rows))):
        lanes = slice(0, cut) if j == 0 else slice(cut, cut + rows // 2)
        keep[:, lanes] = totals[j][:, mine] + totals[2 + j][:, mine]
        send[:, lanes] = (totals[j][:, theirs] + totals[2 + j][:, theirs]).astype(BF)


def own_kernel(ids_0, ids_1, lefts, far_in, keep, send, far, *totals):
    far[...] = far_in[...]
    per = lefts.shape[2]
    rows = totals[0].shape[1]
    for i, ids in enumerate((ids_0, ids_1)):
        spans = lefts.shape[0] // 2
        for b in range(spans):
            left_own = one_hot(ids[LHS : LHS + 1, b * per : (b + 1) * per], rows)
            add = dot_nt(lefts[i * spans + b], left_own)
            if b == 0:
                totals[i][...] = add
            else:
                totals[i][...] += add
    mine, theirs = halves(rows)
    keep[...] = totals[0][:, mine] + totals[1][:, mine]
    send[...] = (totals[0][:, theirs] + totals[1][:, theirs]).astype(BF)


def pair_kernel(keep, got, hot, far):
    cut = hot.shape[1]
    hot[...] = (keep[:, :cut] + got[:, :cut].astype(F32)).astype(BF)
    part = far.shape[0]
    at = pl.ds(pl.multiple_of(lax.axis_index("rep") // 2 * (hot.shape[0] - part), 16), part)
    far[...] = (keep[at, cut:] + got[at, cut:].astype(F32)).astype(BF)


def add_kernel(one, other, out):
    out[...] = (one[...].astype(F32) + other[...].astype(F32)).astype(BF)


def own_sum_kernel(keep, got, far, far_other, out):
    first = lax.axis_index("rep") // 2 == 0
    low = jnp.where(first, far[...].astype(F32), far_other[...].astype(F32))
    high = jnp.where(first, far_other[...].astype(F32), far[...].astype(F32))
    part = low.shape[0]
    over = 2 * part - out.shape[0]
    total = keep[...] + got[...].astype(F32)
    out[:part] = total[:part] + low
    out[part:] = total[part:] + high[over:]


def whole_kernel(own, one, other, out):
    cut = own.shape[1]
    out[:, :cut] = own[...]
    out[:, cut:] = one[...].astype(F32) + other[...].astype(F32)


def adagrad(weights, accum, grad):
    new = accum + jnp.sum(grad * grad, axis=0, keepdims=True) / grad.shape[0]
    return weights - LEARN_RATE * grad / jnp.sqrt(new), new


def near_update_kernel(grads, emb, acc, hot, hot_acc, done, done_acc, rest, rest_acc):
    cut = grads.shape[1] // 2
    mine, theirs = halves(2 * cut)
    for i, (w, a) in enumerate(((emb, acc), (hot, hot_acc))):
        lanes = slice(i * cut, (i + 1) * cut)
        done[:, lanes], done_acc[:, lanes] = adagrad(w[:, mine], a[:, mine], grads[:, lanes])
        rest[:, lanes] = w[:, theirs]
        rest_acc[:, lanes] = a[:, theirs]


def far_update_kernel(grads, done, done_acc, rest, rest_acc, emb, acc, hot, hot_acc):
    cut = grads.shape[1] // 2
    mine, theirs = halves(2 * cut)
    for i, (w, a) in enumerate(((emb, acc), (hot, hot_acc))):
        lanes = slice(i * cut, (i + 1) * cut)
        w[:, mine] = done[:, lanes]
        a[:, mine] = done_acc[:, lanes]
        w[:, theirs], a[:, theirs] = adagrad(rest[:, lanes], rest_acc[:, lanes], grads[:, lanes])


def shifted(block, axis, distance):
    size = lax.axis_size(axis)
    return lax.ppermute(block, axis, [((i - distance) % size, i) for i in range(size)])


def swapped(block, bit):
    return lax.ppermute(block, "rep", [(i, i ^ bit) for i in range(lax.axis_size("rep"))])


def struct(shape, dtype):
    return jax.ShapeDtypeStruct(shape, dtype)


def bucket(fetch, home, count, lhs, rhs, rel_ids, neg, emb, hot, rel):
    width, rows = emb.shape
    hot_rows = hot.shape[1]
    edges = lhs.shape[1]
    spans, n_negs = neg.shape[1:]
    per = edges // spans
    blocks = 2 * spans
    emb_half, ids = call(
        pack_kernel,
        (struct((width, rows // 2), BF), struct((8, edges), jnp.int32)),
        n_in=7,
        anywhere=(5, 6),
    )(emb, lhs, rhs, rel_ids, neg, hot, rel)
    far_half = fetch(emb_half)
    ids = call(live_kernel, struct(ids.shape, jnp.int32), n_in=2, smem=(0,))(count, ids)
    other = swapped(ids, 2)
    columns = (
        struct((spans, width, per), BF),
        struct((spans, width, per), F32),
        struct((spans, rows, 128), F32),
    )
    table, rel_parts, *mine = call(
        first_kernel,
        (struct((width, rows + hot_rows), BF), struct((width, 2 * rel.shape[1]), BF), *columns),
        n_in=4,
    )(emb, hot, rel, ids)
    far_half = call(relay_kernel, struct(far_half.shape, BF), n_in=3, anywhere=(1, 2))(
        far_half, table, other
    )
    far_rest = swapped(far_half, 1)
    theirs = call(second_kernel, columns, n_in=3)(table, rel_parts, other)
    hot_half = struct((width, hot_rows // 2), BF)
    row_half = struct((width, rows // 2), BF)
    both = (width, hot_rows // 2 + rows // 2)
    lefts, keep, send = call(
        functools.partial(edges_kernel, n_negs),
        (struct((blocks, width, per), BF), struct(both, F32), struct(both, BF)),
        scratch=[pltpu.VMEM((width, rows), BF)]
        + [pltpu.VMEM((width, hot_rows), F32), pltpu.VMEM((width, rows), F32)] * 2,
        n_in=10,
    )(far_half, far_rest, ids, *mine, other, *theirs)
    part = struct((-(-width // 32) * 16, rows // 2), BF)
    hot_sum, far_sum = call(pair_kernel, (hot_half, part), n_in=2)(keep, swapped(send, 1))
    own_keep, own_send, far_sum = call(
        own_kernel,
        (struct(row_half.shape, F32), row_half, part),
        scratch=[pltpu.VMEM((width, rows), F32)] * 2,
        n_in=4,
    )(ids, other, lefts, far_sum)
    arrived = home(far_sum)
    arrived_other = swapped(arrived, 2)
    own_got = swapped(own_send, 1)
    size = lax.axis_size("dom")
    for digit in range(size.bit_length() - 1):
        if digit > 0:
            hot_sum = call(add_kernel, hot_half, n_in=2)(hot_sum, hot_got)
        route = [(i, i ^ (1 << digit)) for i in range(size)]
        hot_got = lax.ppermute(hot_sum, "dom", route)
    own = call(own_sum_kernel, struct(row_half.shape, F32), n_in=4)(
        own_keep, own_got, arrived, arrived_other
    )
    return call(whole_kernel, struct((width, rows // 2 + hot_rows // 2), F32), n_in=3)(
        own, hot_sum, hot_got
    )


def four_workers(offset, arrays):
    def branch(shift):
        return functools.partial(
            bucket,
            lambda block: shifted(block, "dom", -shift),
            lambda block: shifted(block, "dom", shift),
        )

    return lax.switch(offset - 1, [branch(1), branch(2), branch(3)], *arrays)


def digit_set(offset, digit):
    return offset // (1 << digit) % 2 == 1


def many_workers(offset, arrays):
    size = lax.axis_size("dom")
    digits = size.bit_length() - 1

    def moved(block, sign):
        for digit in range(digits):
            block = jnp.where(
                digit_set(offset, digit), shifted(block, "dom", sign * (1 << digit)), block
            )
        return block

    return bucket(
        lambda block: moved(block, -1), lambda block: moved(block, 1), *arrays
    )


def body(
    plan, edge_lhs, edge_rhs, edge_rel, edge_count, negatives, emb, acc, hot_emb, hot_acc, relations
):
    emb, acc, hot, hot_acc, rel = emb.T, acc[None, :], hot_emb.T, hot_acc[None, :], relations.T
    workers = lax.axis_size("dom")
    offset = (plan[0] - lax.axis_index("dom")) % workers
    run = four_workers if workers == 4 else many_workers
    mine = run(offset, (edge_count, edge_lhs, edge_rhs, edge_rel, negatives, emb, hot, rel))
    theirs = swapped(mine, 1)
    half, half_acc = struct(mine.shape, F32), struct((1, mine.shape[1]), F32)
    ready = call(near_update_kernel, (half, half_acc, half, half_acc), n_in=5)(
        mine, emb, acc, hot, hot_acc
    )
    new_emb, new_acc, new_hot, new_hot_acc = call(
        far_update_kernel, tuple(struct(x.shape, F32) for x in (emb, acc, hot, hot_acc)), n_in=5
    )(theirs, *ready)
    return (new_emb.T, new_acc[0], new_hot.T, new_hot_acc[0])


def solution(mesh):
    placed = (
        P("dom"),
        P(("groups", "dom"), "rep"),
        P(("groups", "dom"), "rep"),
        P(("groups", "dom"), "rep"),
        P(("groups", "dom", "rep")),
        P(("groups", "dom"), "rep", None),
        P(("groups", "dom"), None),
        P(("groups", "dom")),
        P("groups", None),
        P("groups"),
        P("groups", None),
    )
    return jax.shard_map(
        body,
        mesh=mesh,
        in_specs=placed,
        out_specs=(
            P(("groups", "dom"), None),
            P(("groups", "dom")),
            P("groups", None),
            P("groups"),
        ),
        check_vma=False,
    )
```

```python
import functools

import jax
import jax.numpy as jnp
from jax import lax
from jax.experimental import pallas as pl
from jax.experimental.pallas import tpu as pltpu
from jax.sharding import PartitionSpec as P

LEARN_RATE = 0.5
BF = jnp.bfloat16
F32 = jnp.float32
LHS, RHS, REL, NEG, LIVE = 0, 1, 2, 3, 5
VMEM_LIMIT = 24 * 1024 * 1024


def call(kernel, out_shape, n_in, scratch=(), anywhere=(), smem=()):
    spaces = [
        pltpu.SMEM if i in smem else pl.ANY if i in anywhere else pltpu.VMEM for i in range(n_in)
    ]
    return pl.pallas_call(
        kernel,
        out_shape=out_shape,
        in_specs=[pl.BlockSpec(memory_space=space) for space in spaces],
        scratch_shapes=list(scratch),
        compiler_params=pltpu.CompilerParams(vmem_limit_bytes=VMEM_LIMIT),
        cost_estimate=pl.CostEstimate(flops=1, bytes_accessed=1, transcendentals=0),
    )


def dot_nt(a, b):
    return lax.dot_general(a, b, (((1,), (1,)), ((), ())), preferred_element_type=F32)


def dot_nn(a, b):
    return jnp.dot(a, b, preferred_element_type=F32)


def one_hot(ids, count):
    rows = lax.broadcasted_iota(jnp.int32, (count, ids.shape[1]), 0).astype(jnp.int16)
    return jnp.where(rows == ids.astype(jnp.int16), jnp.ones((), BF), jnp.zeros((), BF))


def halves(axis_size):
    core = lax.axis_index("rep") % 2
    cut = axis_size // 2
    return [pl.ds(pl.multiple_of(c * cut, cut), cut) for c in (core, 1 - core)]


def pack_kernel(emb, lhs, rhs, rel, neg, hot, relations, half, ids):
    del hot, relations
    half[...] = emb[:, halves(emb.shape[1])[0]].astype(BF)
    ids[...] = jnp.full(ids.shape, -1, jnp.int32)
    ids[LHS : LHS + 1, :] = lhs[...]
    ids[RHS : RHS + 1, :] = rhs[...]
    ids[REL : REL + 1, :] = rel[...]
    ids[NEG : NEG + 2, 0 : neg.shape[2]] = neg[0]


def live_kernel(count, ids, out):
    out[...] = ids[...]
    out[LIVE : LIVE + 1, :] = jnp.full((1, ids.shape[1]), count[0], jnp.int32)


def count_rows(ids, counts):
    spans, rows, _ = counts.shape
    for b in range(spans):
        named = ids[NEG + b : NEG + b + 1, :]
        row_ids = lax.broadcasted_iota(jnp.int32, (rows, 128), 0)
        times = jnp.zeros((rows, 128), F32)
        for start in range(0, named.shape[1], 128):
            times += jnp.where(row_ids == named[:, start : start + 128], 1.0, 0.0)
        counts[b] = jnp.broadcast_to(jnp.sum(times, axis=1, keepdims=True), times.shape)


def list_columns(ids, table, rel_parts, query, rel_cols):
    spans, width, per = query.shape
    half = width // 2
    n_rel = rel_parts.shape[1] // 2
    rel_hot = one_hot(ids[REL : REL + 1, :], n_rel)
    rel_all = dot_nn(rel_parts[:, :n_rel], rel_hot) + dot_nn(rel_parts[:, n_rel:], rel_hot)
    left_all = dot_nn(table[...], one_hot(ids[LHS : LHS + 1, :], table.shape[1]))
    for b in range(spans):
        lanes = slice(b * per, (b + 1) * per)
        left, rel_col = left_all[:, lanes], rel_all[:, lanes]
        rel_cols[b] = rel_col
        l_re, l_im = left[:half], left[half:]
        r_re, r_im = rel_col[:half], rel_col[half:]
        query[b, :half] = (l_re * r_re - l_im * r_im).astype(BF)
        query[b, half:] = (l_re * r_im + l_im * r_re).astype(BF)


def first_kernel(emb, hot, rel, ids, table, rel_parts, query, rel_cols, counts):
    count_rows(ids, counts)
    rows = emb.shape[1]
    table[:, :rows] = emb[...].astype(BF)
    table[:, rows:] = hot[...].astype(BF)
    n_rel = rel.shape[1]
    high = rel[...].astype(BF)
    rel_parts[:, :n_rel] = high
    rel_parts[:, n_rel:] = (rel[...] - high.astype(F32)).astype(BF)
    list_columns(ids, table, rel_parts, query, rel_cols)


def second_kernel(table, rel_parts, ids, query, rel_cols, counts):
    count_rows(ids, counts)
    list_columns(ids, table, rel_parts, query, rel_cols)


def relay_kernel(one, after, other, out):
    del after, other
    out[...] = one[...]


def edges_kernel(n_negs, far_half, far_rest, *refs):
    lists = (refs[0:4], refs[4:8])
    lefts, keep, send, far_keep, far_send, far, *totals = refs[8:]
    mine, theirs = halves(far.shape[1])
    far[:, mine] = far_half[...]
    far[:, theirs] = far_rest[...]
    rows = far.shape[1]
    hot_rows = totals[0].shape[1]
    far_t = far[...].astype(F32).T.astype(BF)
    work = []
    for i, (ids, query, rel_cols, counts) in enumerate(lists):
        for b in range(query.shape[0]):
            work.append((i, b, dot_nn(far_t, query[b])))
    spans, width, per = lists[0][1].shape
    half = width // 2
    row_ids = lax.broadcasted_iota(jnp.int32, (rows, per), 0)
    done = []
    for i, b, scores in work:
        ids, query, rel_cols, counts = lists[i]
        lanes = slice(b * per, (b + 1) * per)
        right = row_ids == ids[RHS : RHS + 1, lanes]
        place = lax.broadcasted_iota(jnp.int32, (1, per), 1) + b * per
        mask = jnp.where(place < ids[LIVE : LIVE + 1, lanes], 1.0, 0.0)
        chance = 0.5 * jnp.tanh(0.5 * scores) + 0.5
        times = jnp.concatenate([counts[b]] * (per // 128), axis=1)
        grad = (chance * (mask / n_negs)).astype(BF).astype(F32) * times
        grad = (grad + jnp.where(right, (chance - 1.0) * mask, 0.0)).astype(BF)
        done.append((i, b, grad))
    for i, b, grad in done:
        ids, query, rel_cols, counts = lists[i]
        at = i * spans + b
        lanes = slice(b * per, (b + 1) * per)
        gq = dot_nn(far[...], grad)
        r_re, r_im = rel_cols[b, :half], rel_cols[b, half:]
        g_re, g_im = gq[:half], gq[half:]
        lefts[at, :half] = (g_re * r_re + g_im * r_im).astype(BF)
        lefts[at, half:] = (g_im * r_re - g_re * r_im).astype(BF)
        add_far = dot_nt(query[b], grad)
        hot_total, far_total = totals[2 * i : 2 * i + 2]
        if b == 0:
            far_total[...] = add_far
        else:
            far_total[...] += add_far
    for i, b, grad in done:
        ids, query, rel_cols, counts = lists[i]
        at = i * spans + b
        lanes = slice(b * per, (b + 1) * per)
        hot_total, far_total = totals[2 * i : 2 * i + 2]
        left_hot = one_hot(ids[LHS : LHS + 1, lanes] - rows, hot_rows)
        add_hot = dot_nt(lefts[at], left_hot)
        if b == 0:
            hot_total[...] = add_hot
        else:
            hot_total[...] += add_hot
    outs = ((keep, send), (far_keep, far_send))
    for j, (mine, theirs) in enumerate((halves(hot_rows), halves(rows))):
        outs[j][0][...] = totals[j][:, mine] + totals[2 + j][:, mine]
        outs[j][1][...] = (totals[j][:, theirs] + totals[2 + j][:, theirs]).astype(BF)


def own_kernel(ids_0, ids_1, lefts, far_in, keep, send, far, *totals):
    far[...] = far_in[...]
    per = lefts.shape[2]
    rows = totals[0].shape[1]
    for i, ids in enumerate((ids_0, ids_1)):
        spans = lefts.shape[0] // 2
        for b in range(spans):
            left_own = one_hot(ids[LHS : LHS + 1, b * per : (b + 1) * per], rows)
            add = dot_nt(lefts[i * spans + b], left_own)
            if b == 0:
                totals[i][...] = add
            else:
                totals[i][...] += add
    mine, theirs = halves(rows)
    keep[...] = totals[0][:, mine] + totals[1][:, mine]
    send[...] = (totals[0][:, theirs] + totals[1][:, theirs]).astype(BF)


def hot_pair_kernel(keep, got, hot):
    hot[...] = (keep[...] + got[...].astype(F32)).astype(BF)


def far_pair_kernel(keep, got, far):
    part = far.shape[0]
    at = pl.ds(pl.multiple_of(lax.axis_index("rep") // 2 * (keep.shape[0] - part), 16), part)
    far[...] = (keep[at, :] + got[at, :].astype(F32)).astype(BF)


def add_kernel(one, other, out):
    out[...] = (one[...].astype(F32) + other[...].astype(F32)).astype(BF)


def own_sum_kernel(keep, got, far, far_other, out):
    first = lax.axis_index("rep") // 2 == 0
    low = jnp.where(first, far[...].astype(F32), far_other[...].astype(F32))
    high = jnp.where(first, far_other[...].astype(F32), far[...].astype(F32))
    part = low.shape[0]
    over = 2 * part - out.shape[0]
    total = keep[...] + got[...].astype(F32)
    out[:part] = total[:part] + low
    out[part:] = total[part:] + high[over:]


def whole_kernel(own, one, other, out):
    cut = own.shape[1]
    out[:, :cut] = own[...]
    out[:, cut:] = one[...].astype(F32) + other[...].astype(F32)


def adagrad(weights, accum, grad):
    new = accum + jnp.sum(grad * grad, axis=0, keepdims=True) / grad.shape[0]
    return weights - LEARN_RATE * grad / jnp.sqrt(new), new


def near_update_kernel(grads, emb, acc, hot, hot_acc, done, done_acc, rest, rest_acc):
    cut = grads.shape[1] // 2
    mine, theirs = halves(2 * cut)
    for i, (w, a) in enumerate(((emb, acc), (hot, hot_acc))):
        lanes = slice(i * cut, (i + 1) * cut)
        done[:, lanes], done_acc[:, lanes] = adagrad(w[:, mine], a[:, mine], grads[:, lanes])
        rest[:, lanes] = w[:, theirs]
        rest_acc[:, lanes] = a[:, theirs]


def far_update_kernel(grads, done, done_acc, rest, rest_acc, emb, acc, hot, hot_acc):
    cut = grads.shape[1] // 2
    mine, theirs = halves(2 * cut)
    for i, (w, a) in enumerate(((emb, acc), (hot, hot_acc))):
        lanes = slice(i * cut, (i + 1) * cut)
        w[:, mine] = done[:, lanes]
        a[:, mine] = done_acc[:, lanes]
        w[:, theirs], a[:, theirs] = adagrad(rest[:, lanes], rest_acc[:, lanes], grads[:, lanes])


def shifted(block, axis, distance):
    size = lax.axis_size(axis)
    return lax.ppermute(block, axis, [((i - distance) % size, i) for i in range(size)])


def swapped(block, bit):
    return lax.ppermute(block, "rep", [(i, i ^ bit) for i in range(lax.axis_size("rep"))])


def struct(shape, dtype):
    return jax.ShapeDtypeStruct(shape, dtype)


def bucket(fetch, home, count, lhs, rhs, rel_ids, neg, emb, hot, rel):
    width, rows = emb.shape
    hot_rows = hot.shape[1]
    edges = lhs.shape[1]
    spans, n_negs = neg.shape[1:]
    per = edges // spans
    blocks = 2 * spans
    emb_half, ids = call(
        pack_kernel,
        (struct((width, rows // 2), BF), struct((8, edges), jnp.int32)),
        n_in=7,
        anywhere=(5, 6),
    )(emb, lhs, rhs, rel_ids, neg, hot, rel)
    far_half = fetch(emb_half)
    ids = call(live_kernel, struct(ids.shape, jnp.int32), n_in=2, smem=(0,))(count, ids)
    other = swapped(ids, 2)
    columns = (
        struct((spans, width, per), BF),
        struct((spans, width, per), F32),
        struct((spans, rows, 128), F32),
    )
    table, rel_parts, *mine = call(
        first_kernel,
        (struct((width, rows + hot_rows), BF), struct((width, 2 * rel.shape[1]), BF), *columns),
        n_in=4,
    )(emb, hot, rel, ids)
    far_half = call(relay_kernel, struct(far_half.shape, BF), n_in=3, anywhere=(1, 2))(
        far_half, table, other
    )
    far_rest = swapped(far_half, 1)
    theirs = call(second_kernel, columns, n_in=3)(table, rel_parts, other)
    hot_half = struct((width, hot_rows // 2), BF)
    row_half = struct((width, rows // 2), BF)
    lefts, keep, send, far_keep, far_send = call(
        functools.partial(edges_kernel, n_negs),
        (struct((blocks, width, per), BF), struct(hot_half.shape, F32), hot_half, struct(row_half.shape, F32), row_half),
        scratch=[pltpu.VMEM((width, rows), BF)]
        + [pltpu.VMEM((width, hot_rows), F32), pltpu.VMEM((width, rows), F32)] * 2,
        n_in=10,
    )(far_half, far_rest, ids, *mine, other, *theirs)
    part = struct((-(-width // 32) * 16, rows // 2), BF)
    hot_sum = call(hot_pair_kernel, hot_half, n_in=2)(keep, swapped(send, 1))
    far_sum = call(far_pair_kernel, part, n_in=2)(far_keep, swapped(far_send, 1))
    own_keep, own_send, far_sum = call(
        own_kernel,
        (struct(row_half.shape, F32), row_half, part),
        scratch=[pltpu.VMEM((width, rows), F32)] * 2,
        n_in=4,
    )(ids, other, lefts, far_sum)
    arrived = home(far_sum)
    arrived_other = swapped(arrived, 2)
    own_got = swapped(own_send, 1)
    size = lax.axis_size("dom")
    for digit in range(size.bit_length() - 1):
        if digit > 0:
            hot_sum = call(add_kernel, hot_half, n_in=2)(hot_sum, hot_got)
        route = [(i, i ^ (1 << digit)) for i in range(size)]
        hot_got = lax.ppermute(hot_sum, "dom", route)
    own = call(own_sum_kernel, struct(row_half.shape, F32), n_in=4)(
        own_keep, own_got, arrived, arrived_other
    )
    return call(whole_kernel, struct((width, rows // 2 + hot_rows // 2), F32), n_in=3)(
        own, hot_sum, hot_got
    )


def four_workers(offset, arrays):
    def branch(shift):
        return functools.partial(
            bucket,
            lambda block: shifted(block, "dom", -shift),
            lambda block: shifted(block, "dom", shift),
        )

    return lax.switch(offset - 1, [branch(1), branch(2), branch(3)], *arrays)


def digit_set(offset, digit):
    return offset // (1 << digit) % 2 == 1


def many_workers(offset, arrays):
    size = lax.axis_size("dom")
    digits = size.bit_length() - 1

    def moved(block, sign):
        for digit in range(digits):
            block = jnp.where(
                digit_set(offset, digit), shifted(block, "dom", sign * (1 << digit)), block
            )
        return block

    return bucket(
        lambda block: moved(block, -1), lambda block: moved(block, 1), *arrays
    )


def body(
    plan, edge_lhs, edge_rhs, edge_rel, edge_count, negatives, emb, acc, hot_emb, hot_acc, relations
):
    emb, acc, hot, hot_acc, rel = emb.T, acc[None, :], hot_emb.T, hot_acc[None, :], relations.T
    workers = lax.axis_size("dom")
    offset = (plan[0] - lax.axis_index("dom")) % workers
    run = four_workers if workers == 4 else many_workers
    mine = run(offset, (edge_count, edge_lhs, edge_rhs, edge_rel, negatives, emb, hot, rel))
    theirs = swapped(mine, 1)
    half, half_acc = struct(mine.shape, F32), struct((1, mine.shape[1]), F32)
    ready = call(near_update_kernel, (half, half_acc, half, half_acc), n_in=5)(
        mine, emb, acc, hot, hot_acc
    )
    new_emb, new_acc, new_hot, new_hot_acc = call(
        far_update_kernel, tuple(struct(x.shape, F32) for x in (emb, acc, hot, hot_acc)), n_in=5
    )(theirs, *ready)
    return (new_emb.T, new_acc[0], new_hot.T, new_hot_acc[0])


def solution(mesh):
    placed = (
        P("dom"),
        P(("groups", "dom"), "rep"),
        P(("groups", "dom"), "rep"),
        P(("groups", "dom"), "rep"),
        P(("groups", "dom", "rep")),
        P(("groups", "dom"), "rep", None),
        P(("groups", "dom"), None),
        P(("groups", "dom")),
        P("groups", None),
        P("groups"),
        P("groups", None),
    )
    return jax.shard_map(
        body,
        mesh=mesh,
        in_specs=placed,
        out_specs=(
            P(("groups", "dom"), None),
            P(("groups", "dom")),
            P("groups", None),
            P("groups"),
        ),
        check_vma=False,
    )
```
